256 devices in a mesh: tx: 8 (over z), ty: 32 (over y, x, core).
Axes of the slice: x: 4, y: 4, z: 8, core: 2. Of those that a mesh axis runs over, the one named last changes fastest.
Arguments:
- signal: bfloat16 [262144, 256], P(('tx', 'ty')), may hold values from -6 to 6
- sketch: bfloat16 [64, 16384], replicated, may hold values from -0.046875 to 0.046875
Outputs:
- basis_t: float32 [64, 262144], P(None, ('tx', 'ty'))
- projected: float32 [64, 16384], P(None, ('tx', 'ty'))
The draws below stay inside these ranges and needn't reach their ends.
All inputs are finite; a program needn't handle non-finite values.
Results may differ from the reference program's by a relative error of at most 0.00071.
Values may be sent and summed in bfloat16 or wider, within the bound.
A program may use at most 128 MiB of HBM per device.

```python
import math
import jax
import jax.numpy as jnp
from jax import lax

CHANNELS = 256
LAGS = 64
RANK = 64
SAMP_DEV = 1024
SAMPLES = 262144


def levels(key, shape, cuts, low, largest):
    def one(dim, shards_of):
        draws = jax.random.uniform(jax.random.fold_in(jax.random.fold_in(key, 6), dim), (shards_of,), jnp.float32, low / len(cuts), largest / len(cuts))
        return jnp.repeat(jnp.exp(draws), shape[dim] // shards_of).reshape((-1,) + (1,) * (len(shape) - dim - 1))

    factor_of = one(*cuts[0])
    for cut in cuts[1:]:
        factor_of = factor_of * one(*cut)
    return factor_of


def scatter_about(own_key, dims, spread, reach, cuts=(), kind=jnp.bfloat16):
    entries = jax.random.normal(own_key, dims, jnp.float32) * spread
    if len(cuts) > 0:
        entries = levels(own_key, dims, cuts, -0.22, 0.18) * entries
    return jnp.clip(entries, min=-reach, max=reach).astype(kind)


def setup_inputs(seed: int = 0) -> dict:
    key_of = jax.random.split(jax.random.key(seed), 3)
    signal = scatter_about(key_of[0], (SAMPLES, CHANNELS), 1.0, 6.0, ((0, 256),))
    sketch = scatter_about(key_of[1], (RANK, LAGS * CHANNELS), (LAGS * CHANNELS) ** -0.5, 0.046875)
    return dict(signal=signal, sketch=sketch)


def sketch_rows(extended, sketch):
    span = extended.shape[0] - LAGS + 1
    lagged = jnp.dot(sketch.reshape(RANK * LAGS, CHANNELS).astype(jnp.float32), extended.astype(jnp.float32).T, precision=lax.Precision.HIGHEST)
    lagged = lagged.reshape(RANK, LAGS, extended.shape[0])
    sketched = lagged[:, 0, 0:span]
    for lag_index in range(1, LAGS):
        sketched = sketched + lagged[:, lag_index, lag_index:lag_index + span]
    return sketched

def shifted_stack(rounded):
    padded = jnp.pad(rounded, ((0, 0), (LAGS - 1, LAGS - 1)))
    length = rounded.shape[1] + LAGS - 1
    return jnp.stack([padded[:, LAGS - 1 - lag_index:LAGS - 1 - lag_index + length] for lag_index in range(LAGS)], axis=1)

def project_rows(rounded, extended):
    shifted = shifted_stack(rounded).reshape(RANK * LAGS, extended.shape[0]).astype(jnp.float32)
    product = jnp.dot(shifted, extended.astype(jnp.float32), precision=lax.Precision.HIGHEST)
    return product.reshape(RANK, LAGS * CHANNELS)

def reference(signal, sketch):
    padded = jnp.concatenate([signal, jnp.zeros((LAGS - 1, CHANNELS), jnp.bfloat16)], axis=0)
    blocks = SAMPLES // SAMP_DEV

    def one_block(index):
        extended = lax.dynamic_slice_in_dim(padded, index * SAMP_DEV, SAMP_DEV + LAGS - 1, 0)
        return sketch_rows(extended, sketch)
    sketched = lax.map(one_block, jnp.arange(blocks, dtype=jnp.int32))
    sketched = jnp.transpose(sketched, (1, 0, 2)).reshape(RANK, SAMPLES)
    gram = jnp.dot(sketched, sketched.T, precision=lax.Precision.HIGHEST) / SAMPLES
    triangle = jnp.linalg.cholesky(gram)
    inverse = lax.linalg.triangular_solve(triangle, jnp.eye(RANK, dtype=triangle.dtype), left_side=True, lower=True)
    basis_t = jnp.dot(inverse, sketched, precision=lax.Precision.HIGHEST)
    rounded = basis_t.astype(jnp.bfloat16)

    def add_block(carry, index):
        piece = lax.dynamic_slice_in_dim(rounded, index * SAMP_DEV, SAMP_DEV, 1)
        extended = lax.dynamic_slice_in_dim(padded, index * SAMP_DEV, SAMP_DEV + LAGS - 1, 0)
        return (carry + project_rows(piece, extended), None)
    projected, _ = lax.scan(add_block, jnp.zeros((RANK, LAGS * CHANNELS), jnp.float32), jnp.arange(blocks, dtype=jnp.int32))
    return (basis_t, projected / math.sqrt(SAMPLES))
```

```python
import math

import jax
import jax.numpy as jnp
from jax import lax
from jax.experimental import pallas as pl
from jax.experimental.pallas import tpu as pltpu
from jax.sharding import PartitionSpec as P

MESH = pl.DeviceIdType.MESH
F32 = jnp.float32
BF16 = jnp.bfloat16
HIGH = lax.Precision.HIGHEST
NT = (((1,), (1,)), ((), ()))

ROWS = 1024
CH = 256
RANK = 64
LAGS = 64
DEPTH = 2176
SAMPLES = 262144


def lower_inverse(gram):
    row_of = lax.broadcasted_iota(jnp.int32, (8, 128), 0)
    lane_of = lax.broadcasted_iota(jnp.int32, (8, 128), 1)
    blocks = []
    for g in range(8):
        eye = jnp.where(lane_of == row_of + (64 + 8 * g), 1.0, 0.0).astype(F32)
        blocks.append(jnp.concatenate([gram[8 * g : 8 * g + 8], eye[:, 64:]], axis=1))
    for k in range(RANK - 1):
        own, at = divmod(k, 8)
        row = blocks[own][at : at + 1, :]
        scaled = row / row[:, k : k + 1]
        for g in range(own, 8):
            col = blocks[g][:, k : k + 1]
            if g == own:
                col = jnp.where(row_of[:, 0:1] > at, col, 0.0)
            blocks[g] = blocks[g] - col * scaled
    out = []
    for g in range(8):
        pivot = jnp.sum(jnp.where(lane_of == row_of + 8 * g, blocks[g], 0.0), axis=1, keepdims=True)
        out.append(blocks[g][:, 64:] * (1.0 / jnp.sqrt(pivot)))
    return jnp.concatenate(out, axis=0)


def folded(block):
    return jnp.concatenate([block[0:32], block[32:64]], axis=1)


def unfolded(block):
    return jnp.concatenate([block[:, 0:64], block[:, 64:128]], axis=0)


def kernel(
    signal,
    sketch,
    basis,
    proj,
    sk_v,
    ext,
    xf,
    xs,
    pair,
    tail,
    pf,
    bs,
    uu,
    vv,
    skl,
    ss,
    gs,
    gx,
    gy,
    gz,
    ya,
    yb,
    ra,
    rb,
    sa,
    sb,
    r2a,
    r2b,
    zp,
    rz,
    local_sem,
    send_sem,
    recv_sem,
):
    z = lax.axis_index("tx")
    ty = lax.axis_index("ty")
    y = ty // 8
    x = (ty // 2) % 4
    core = ty % 2
    me = z * 32 + ty

    def along(offset):
        index = (me + offset + 256) % 256
        return (index // 32, index % 32)

    def x_peer(k):
        return (z, y * 8 + ((x + k + 4) % 4) * 2 + core)

    def y_peer(k):
        return (z, ((y + k + 4) % 4) * 8 + x * 2 + core)

    def z_peer(k):
        return ((z + k + 8) % 8, ty)

    twin = (z, ty + 1 - 2 * core)

    def own_quarters(rows):
        first = jnp.concatenate([rows[:, 0:64], rows[:, 128:192]], axis=1)
        second = jnp.concatenate([rows[:, 64:128], rows[:, 192:256]], axis=1)
        return jnp.where(core == 0, first, second)

    used = [0]

    def remote(src, dst, device):
        i = used[0]
        used[0] += 1
        return pltpu.make_async_remote_copy(
            src_ref=src,
            dst_ref=dst,
            send_sem=send_sem.at[i],
            recv_sem=recv_sem.at[i],
            device_id=device,
            device_id_type=MESH,
        )

    get_signal = pltpu.make_async_copy(signal, ext.at[pl.ds(0, ROWS)], local_sem.at[0])
    get_sketch = pltpu.make_async_copy(sketch, sk_v, local_sem.at[1])
    own_start = pl.multiple_of(core * ROWS, ROWS)
    twin_start = pl.multiple_of(ROWS - core * ROWS, ROWS)
    get_signal.start()
    get_sketch.start()

    barrier = pltpu.get_barrier_semaphore()
    sources = [along(1), along(2), twin]
    sources += [x_peer(-k) for k in range(1, 4)]
    sources += [y_peer(-k) for k in range(1, 4)]
    sources += [z_peer(-k) for k in range(1, 8)]
    for source in sources:
        pl.semaphore_signal(barrier, inc=1, device_id=source, device_id_type=MESH)
    pl.semaphore_wait(barrier, len(sources))

    halo_copy = remote(signal.at[pl.ds(0, 64)], ext.at[pl.ds(ROWS, 64)], along(-1))
    halo_copy.start()
    pair_copy = remote(signal, pair, twin)
    pair_copy.start()
    tail_copy = remote(signal.at[pl.ds(0, 64)], tail, along(-2))
    tail_copy.start()

    get_signal.wait()
    xf[pl.ds(1088, 64)] = jnp.zeros((64, CH), F32)

    @pl.loop(0, 16)
    def _(i):
        at = pl.multiple_of(i * 64, 64)
        xf[pl.ds(at, 64)] = ext[pl.ds(at, 64)].astype(F32)

    halo_copy.wait_recv()

    @pl.when(me == 255)
    def _():
        ext[pl.ds(ROWS, 64)] = jnp.zeros((64, CH), BF16)

    xf[pl.ds(ROWS, 64)] = ext[pl.ds(ROWS, 64)].astype(F32)

    @pl.loop(0, 17)
    def _(i):
        at = pl.multiple_of(i * 64, 64)
        near = xf[pl.ds(at, 80)]
        for m in range(1, 4):
            xs[m - 1, pl.ds(at, 64)] = near[4 * m : 4 * m + 64].astype(BF16)

    get_sketch.wait()
    span = 1040
    left = []
    for q in range(16):
        m, at = q % 4, 16 * (q // 4)
        left.append(ext[at : at + span] if m == 0 else xs[m - 1, at : at + span])
    right = [
        jnp.concatenate([sk_v[:, (4 * q + j) * CH : (4 * q + j + 1) * CH] for q in range(16)], axis=1)
        for j in range(4)
    ]
    uu[...] = lax.dot_general(
        jnp.concatenate(left, axis=1), jnp.concatenate(right, axis=0), NT, preferred_element_type=F32
    )
    vv[...] = uu[0:1032, 0:128] + uu[2:1034, 128:256]
    total = vv[0:ROWS] + pltpu.roll(vv[1 : ROWS + 1], 64, axis=1)
    skl[core] = total.T[0:RANK]
    sketched_copy = remote(skl.at[core], skl.at[core], twin)
    sketched_copy.start()

    pair_copy.wait_recv()
    tail_copy.wait_recv()
    last = jnp.where(core == 0, tail[...].astype(F32), xf[pl.ds(ROWS, 64)])
    pf[pl.ds(2048, 64)] = jnp.where(me >= 254, 0.0, own_quarters(last))
    pf[pl.ds(2112, 128)] = jnp.zeros((128, 128), F32)

    @pl.loop(0, 16)
    def _(i):
        at = pl.multiple_of(i * 64, 64)
        pf[pl.ds(own_start + at, 64)] = own_quarters(xf[pl.ds(at, 64)])
        pf[pl.ds(twin_start + at, 64)] = own_quarters(pair[pl.ds(at, 64)].astype(F32))

    @pl.loop(0, 137)
    def _(i):
        at = pl.multiple_of(i * 16, 16)
        near = pf[pl.ds(at, 64)]
        for m in range(4):
            now = near[4 * m : 4 * m + 16]
            later = near[4 * m + 32 : 4 * m + 48]
            low = jnp.concatenate([now[:, 0:64], later[:, 0:64]], axis=1)
            high = jnp.concatenate([now[:, 64:128], later[:, 64:128]], axis=1)
            bs[m, pl.ds(at, 16), 0:128] = low.astype(BF16)
            bs[m, pl.ds(at, 16), 128:256] = high.astype(BF16)

    sketched_copy.wait_recv()
    full = jnp.concatenate([skl[0], skl[1]], axis=1)
    gram = lax.dot_general(full, full, NT, precision=HIGH, preferred_element_type=F32)
    gs[0] = folded(gram)
    gram_x = [remote(gs.at[0], gx.at[k - 1], x_peer(k)) for k in range(1, 4)]
    for copy in gram_x:
        copy.start()

    padded = jnp.concatenate([full, jnp.zeros((RANK, DEPTH - 2048), F32)], axis=1)
    for j in range(4):
        moved = padded if j == 0 else pltpu.roll(padded, j, axis=1)
        high = moved.astype(BF16)
        ss[j * 64 : j * 64 + 64] = high
        ss[256 + j * 64 : 256 + j * 64 + 64] = (moved - high.astype(F32)).astype(BF16)

    def products(half, into):
        @pl.loop(0, 4)
        def _(m):
            both = jnp.dot(ss[...], bs[m, 16 * half : 16 * half + DEPTH], preferred_element_type=F32)
            block = both[0:256] + both[256:512]
            at = pl.ds(pl.multiple_of((m // 2) * 64, 64), 64)
            for j in range(4):
                y_to = (m % 2) * 2 + j // 2
                for x0 in range(2):
                    x_to = (j % 2) * 2 + x0
                    piece = block[j * 64 : j * 64 + 64, x0 * 128 : x0 * 128 + 128]
                    if half == 0:
                        into[x_to, y_to, at] = piece
                    else:
                        into[y_to, x_to, at] = piece

    products(0, ya)
    a_first = [remote(ya.at[(x + k) % 4], ra.at[k - 1], x_peer(k)) for k in range(1, 4)]
    for copy in a_first:
        copy.start()

    for copy in gram_x:
        copy.wait_recv()
    gs[1] = gs[0] + gx[0] + gx[1] + gx[2]
    gram_y = [remote(gs.at[1], gy.at[k - 1], y_peer(k)) for k in range(1, 4)]
    for copy in gram_y:
        copy.start()

    products(1, yb)
    b_first = [remote(yb.at[(y + k) % 4], rb.at[k - 1], y_peer(k)) for k in range(1, 4)]
    for copy in b_first:
        copy.start()

    for copy in gram_y:
        copy.wait_recv()
    gs[2] = gs[1] + gy[0] + gy[1] + gy[2]
    gram_z = [remote(gs.at[2], gz.at[k - 1], z_peer(k)) for k in range(1, 8)]
    for copy in gram_z:
        copy.start()
    for copy in gram_z:
        copy.wait_recv()
    gram_sum = gs[2]
    for k in range(7):
        gram_sum = gram_sum + gz[k]
    inverse = lower_inverse(unfolded(gram_sum) * (1.0 / SAMPLES))
    basis[...] = jnp.dot(inverse, skl[core], precision=HIGH, preferred_element_type=F32)

    for copy in a_first:
        copy.wait_recv()
    sa[...] = ya[x] + ra[0] + ra[1] + ra[2]
    a_second = [remote(sa.at[(y + k) % 4], r2a.at[k - 1], y_peer(k)) for k in range(1, 4)]
    for copy in a_second:
        copy.start()
    for copy in b_first:
        copy.wait_recv()
    sb[...] = yb[y] + rb[0] + rb[1] + rb[2]
    b_second = [remote(sb.at[(x + k) % 4], r2b.at[k - 1], x_peer(k)) for k in range(1, 4)]
    for copy in b_second:
        copy.start()

    def pack(l4, block):
        for l3 in range(2):
            top = block[l3 * 64 : l3 * 64 + 32]
            low = block[l3 * 64 + 32 : l3 * 64 + 64]
            zp[2 * l4 + l3] = jnp.concatenate([top[:, 0:64], low[:, 0:64]], axis=1)
            zp[4 + 2 * l4 + l3] = jnp.concatenate([top[:, 64:128], low[:, 64:128]], axis=1)

    for copy in a_second:
        copy.wait_recv()
    pack(0, sa[y] + r2a[0] + r2a[1] + r2a[2])
    for copy in b_second:
        copy.wait_recv()
    pack(1, sb[x] + r2b[0] + r2b[1] + r2b[2])
    last_copies = [remote(zp.at[(z + k) % 8], rz.at[k - 1], z_peer(k)) for k in range(1, 8)]
    for copy in last_copies:
        copy.start()
    for copy in last_copies:
        copy.wait_recv()
    owned = zp[z]
    for k in range(7):
        owned = owned + rz[k]
    proj[...] = jnp.dot(inverse, unfolded(owned), precision=HIGH, preferred_element_type=F32) * (
        1.0 / math.sqrt(SAMPLES)
    )

    sent = [halo_copy, pair_copy, tail_copy, sketched_copy]
    sent += gram_x + gram_y + gram_z + a_first + b_first + a_second + b_second + last_copies
    for copy in sent:
        copy.wait_send()


COPIES = 4 + 3 + 3 + 7 + 3 + 3 + 3 + 3 + 7


def shards(signal, sketch):
    return pl.pallas_call(
        kernel,
        out_shape=(
            jax.ShapeDtypeStruct((RANK, ROWS), F32),
            jax.ShapeDtypeStruct((RANK, 64), F32),
        ),
        in_specs=[pl.BlockSpec(memory_space=pl.ANY)] * 2,
        out_specs=[pl.BlockSpec(memory_space=pltpu.VMEM)] * 2,
        scratch_shapes=[
            pltpu.VMEM((RANK, LAGS * CH), BF16),
            pltpu.VMEM((1088, CH), BF16),
            pltpu.VMEM((1152, CH), F32),
            pltpu.VMEM((3, 1088, CH), BF16),
            pltpu.VMEM((ROWS, CH), BF16),
            pltpu.VMEM((64, CH), BF16),
            pltpu.VMEM((2240, 128), F32),
            pltpu.VMEM((4, 2192, CH), BF16),
            pltpu.VMEM((1040, CH), F32),
            pltpu.VMEM((1032, 128), F32),
            pltpu.VMEM((2, RANK, ROWS), F32),
            pltpu.VMEM((512, DEPTH), BF16),
            pltpu.VMEM((3, 32, 128), F32),
            pltpu.VMEM((3, 32, 128), F32),
            pltpu.VMEM((3, 32, 128), F32),
            pltpu.VMEM((7, 32, 128), F32),
            pltpu.VMEM((4, 4, 128, 128), F32),
            pltpu.VMEM((4, 4, 128, 128), F32),
            pltpu.VMEM((3, 4, 128, 128), F32),
            pltpu.VMEM((3, 4, 128, 128), F32),
            pltpu.VMEM((4, 128, 128), F32),
            pltpu.VMEM((4, 128, 128), F32),
            pltpu.VMEM((3, 128, 128), F32),
            pltpu.VMEM((3, 128, 128), F32),
            pltpu.VMEM((8, 32, 128), F32),
            pltpu.VMEM((7, 32, 128), F32),
            pltpu.SemaphoreType.DMA((2,)),
            pltpu.SemaphoreType.DMA((COPIES,)),
            pltpu.SemaphoreType.DMA((COPIES,)),
        ],
        compiler_params=pltpu.CompilerParams(
            collective_id=0, has_side_effects=True, vmem_limit_bytes=48 * 2**20
        ),
        name="range_finder",
    )(signal, sketch)


def solution(mesh):
    in_specs = (P(("tx", "ty"), None), P())
    out_specs = (P(None, ("tx", "ty")), P(None, ("tx", "ty")))
    return jax.shard_map(shards, mesh=mesh, in_specs=in_specs, out_specs=out_specs, check_vma=False)
```

```python
import math

import jax
import jax.numpy as jnp
from jax import lax
from jax.experimental import pallas as pl
from jax.experimental.pallas import tpu as pltpu
from jax.sharding import PartitionSpec as P

MESH = pl.DeviceIdType.MESH
F32 = jnp.float32
BF16 = jnp.bfloat16
HIGH = lax.Precision.HIGHEST
NT = (((1,), (1,)), ((), ()))

ROWS = 1024
CH = 256
RANK = 64
LAGS = 64
HALF = 32
TIMES = 2048
DEPTH = 2176
SAMPLES = 262144


def lower_inverse(gram):
    row_of = lax.broadcasted_iota(jnp.int32, (8, 128), 0)
    lane_of = lax.broadcasted_iota(jnp.int32, (8, 128), 1)
    blocks = []
    for g in range(8):
        eye = jnp.where(lane_of == row_of + (64 + 8 * g), 1.0, 0.0).astype(F32)
        blocks.append(jnp.concatenate([gram[8 * g : 8 * g + 8], eye[:, 64:]], axis=1))
    for k in range(RANK - 1):
        own, at = divmod(k, 8)
        row = blocks[own][at : at + 1, :]
        scaled = row / row[:, k : k + 1]
        for g in range(own, 8):
            col = blocks[g][:, k : k + 1]
            if g == own:
                col = jnp.where(row_of[:, 0:1] > at, col, 0.0)
            blocks[g] = blocks[g] - col * scaled
    out = []
    for g in range(8):
        pivot = jnp.sum(jnp.where(lane_of == row_of + 8 * g, blocks[g], 0.0), axis=1, keepdims=True)
        out.append(blocks[g][:, 64:] * (1.0 / jnp.sqrt(pivot)))
    return jnp.concatenate(out, axis=0)


def folded(block):
    n = block.shape[0] // 2
    return jnp.concatenate([block[0:n], block[n:]], axis=1)


def unfolded(block):
    return jnp.concatenate([block[:, 0:64], block[:, 64:128]], axis=0)


class RingSum:
    def __init__(self, remote, blocks, place, right, left, passing, arrived):
        self.blocks, self.place, self.passing, self.arrived = blocks, place, passing, arrived
        self.after, self.before = (place + 1) % 4, (place + 3) % 4
        across = (place + 2) % 4
        self.across_first = remote(blocks.at[across, 0], passing.at[0], right)
        self.across_second = remote(blocks.at[across, 1], passing.at[1], left)
        self.before_first = remote(blocks.at[self.before, 0], arrived.at[1, 0], left)
        self.after_second = remote(blocks.at[self.after, 1], arrived.at[0, 1], right)
        self.after_first = remote(blocks.at[self.after, 0], arrived.at[0, 0], right)
        self.before_second = remote(blocks.at[self.before, 1], arrived.at[1, 1], left)

    def start_first(self):
        self.across_first.start()
        self.before_first.start()

    def start_second(self):
        self.across_second.start()
        self.after_second.start()

    def forward_first(self):
        self.across_first.wait_recv()
        self.blocks[self.after, 0] += self.passing[0]
        self.after_first.start()

    def forward_second(self):
        self.across_second.wait_recv()
        self.blocks[self.before, 1] += self.passing[1]
        self.before_second.start()

    def total_first(self):
        self.before_first.wait_recv()
        self.after_first.wait_recv()
        return self.blocks[self.place, 0] + self.arrived[0, 0] + self.arrived[1, 0]

    def total_second(self):
        self.after_second.wait_recv()
        self.before_second.wait_recv()
        return self.blocks[self.place, 1] + self.arrived[0, 1] + self.arrived[1, 1]


def kernel(
    signal,
    sketch,
    basis,
    proj,
    sk_v,
    xr,
    uu,
    vv,
    vw,
    skl,
    ss,
    gs,
    gx,
    gy,
    gz,
    ya,
    yb,
    fa,
    fb,
    ra,
    rb,
    sa,
    sb,
    ra2,
    rb2,
    zp,
    rz,
    local_sem,
    send_sem,
    recv_sem,
):
    z = lax.axis_index("tx")
    ty = lax.axis_index("ty")
    y = ty // 8
    x = (ty // 2) % 4
    core = ty % 2
    me = z * 32 + ty

    def along(offset):
        index = (me + offset + 256) % 256
        return (index // 32, index % 32)

    def x_peer(k):
        return (z, y * 8 + ((x + k + 4) % 4) * 2 + core)

    def y_peer(k):
        return (z, ((y + k + 4) % 4) * 8 + x * 2 + core)

    def z_peer(k):
        return ((z + k + 8) % 8, ty)

    other = ty + 1 - 2 * core
    twin = (z, other)

    def z_other(k):
        return ((z + k + 8) % 8, other)

    copies = []

    def remote(src, dst, device):
        i = len(copies)
        copies.append(pltpu.make_async_remote_copy(
            src_ref=src,
            dst_ref=dst,
            send_sem=send_sem.at[i],
            recv_sem=recv_sem.at[i],
            device_id=device,
            device_id_type=MESH,
        ))
        return copies[i]

    own_rows = pl.ds(pl.multiple_of(core * ROWS, ROWS), ROWS)
    own_ranks = pl.ds(pl.multiple_of(core * HALF, HALF), HALF)
    get_signal = pltpu.make_async_copy(signal, xr.at[0, own_rows], local_sem.at[0])
    get_sketch = pltpu.make_async_copy(sketch.at[own_ranks], sk_v, local_sem.at[1])
    get_signal.start()
    get_sketch.start()

    barrier = pltpu.get_barrier_semaphore()
    sources = [along(2 - core), twin]
    sources += [x_peer(-k) for k in range(1, 4)]
    sources += [y_peer(-k) for k in range(1, 4)]
    sources += [z_peer(-k) for k in range(1, 8)]
    sources += [z_other(-k) for k in range(1, 8)]
    for source in sources:
        pl.semaphore_signal(barrier, inc=1, device_id=source, device_id_type=MESH)
    pl.semaphore_wait(barrier, len(sources) - 1 + 2 * (1 - core))

    halo_rows = pl.ds(TIMES, 64)
    halo_near = remote(signal.at[pl.ds(0, 64)], xr.at[0, halo_rows], along(-1))
    halo_far = pltpu.make_async_remote_copy(
        src_ref=signal.at[pl.ds(0, 64)],
        dst_ref=xr.at[0, halo_rows],
        send_sem=local_sem.at[2],
        recv_sem=recv_sem.at[0],
        device_id=along(-2),
        device_id_type=MESH,
    )

    @pl.when(core == 0)
    def _():
        halo_near.start()
        halo_far.start()

    pair_copy = remote(signal, xr.at[0, own_rows], twin)
    pair_copy.start()

    for m in range(2):
        xr[m, 2112:2240] = jnp.zeros((128, CH), BF16)
    get_signal.wait()
    pair_copy.wait_recv()

    @pl.loop(0, 15)
    def _(i):
        at = pl.multiple_of(i * 128, 128)
        near = xr[0, pl.ds(at, 144)]
        xr[1, pl.ds(at, 128)] = near[8:136]

    near = xr[0, 1920:2048]
    xr[1, 1920:2032] = near[8:120]

    get_sketch.wait()
    columns = jnp.concatenate(
        [
            jnp.concatenate([sk_v[:, (8 * q + j) * CH : (8 * q + j + 1) * CH] for q in range(8)], axis=1)
            for j in range(8)
        ],
        axis=0,
    )

    def sub_shifted(start, rows):
        moved = [xr[q % 2, 16 * (q // 2) + start : 16 * (q // 2) + start + rows] for q in range(8)]
        uu[start : start + rows] = lax.dot_general(
            jnp.concatenate(moved, axis=1), columns, NT, preferred_element_type=F32
        )

    sub_shifted(0, 1984)
    halo_near.wait_recv()

    @pl.when(me >= 254)
    def _():
        xr[0, halo_rows] = jnp.zeros((64, CH), BF16)

    near = xr[0, 2032:2128]
    xr[1, 2032:2112] = near[8:88]
    sub_shifted(1984, 80)

    vv[...] = uu[0:2056, 0:128] + uu[4:2060, 128:256]
    vw[...] = vv[0:2052] + pltpu.roll(vv[2:2054], 64, axis=1)
    group = lax.broadcasted_iota(jnp.int32, (512, 128), 1) // HALF
    merged = None
    for g in range(4):
        at = g * 512
        part = vw[at : at + 512] + pltpu.roll(vw[at + 1 : at + 513], 96, axis=1)
        merged = part if g == 0 else jnp.where(group == g, pltpu.roll(part, 32 * g, axis=1), merged)
    turned = merged.T
    for g in range(4):
        skl[core, :, g * 512 : g * 512 + 512] = turned[g * HALF : g * HALF + HALF]
    sketched_copy = remote(skl.at[core], skl.at[core], twin)
    sketched_copy.start()

    padded = jnp.concatenate([skl[core], jnp.zeros((HALF, DEPTH - TIMES), F32)], axis=1)
    for j in range(8):
        moved = padded if j == 0 else pltpu.roll(padded, j, axis=1)
        high = moved.astype(BF16)
        ss[j * HALF : j * HALF + HALF] = high
        ss[256 + j * HALF : 256 + j * HALF + HALF] = (moved - high.astype(F32)).astype(BF16)

    def products(z_to, into, x_first):
        @pl.loop(0, 2)
        def _(i):
            right = xr[i, 8 * z_to : 8 * z_to + DEPTH]
            both = jnp.dot(ss[...], right, preferred_element_type=F32)
            block = both[0:256] + both[256:512]
            at = pl.ds(pl.multiple_of(i * HALF, HALF), HALF)
            half = (z_to % 4) // 2
            for j in range(8):
                y_to = j // 2
                for x0 in range(2):
                    x_to = (j % 2) * 2 + x0
                    piece = block[j * HALF : j * HALF + HALF, x0 * 128 : x0 * 128 + 128]
                    if x_first:
                        into[x_to, half, y_to, at] = piece
                    else:
                        into[y_to, half, x_to, at] = piece

    a_one = RingSum(remote, ya, x, x_peer(1), x_peer(-1), fa, ra)
    b_one = RingSum(remote, yb, y, y_peer(1), y_peer(-1), fb, rb)
    products(0, ya, True)
    a_one.start_first()
    products(4, yb, False)
    b_one.start_first()

    sketched_copy.wait_recv()
    full = jnp.concatenate([skl[0], skl[1]], axis=0)
    high = full.astype(BF16)
    rest = full - high.astype(F32)
    middle = rest.astype(BF16)
    low = (rest - middle.astype(F32)).astype(BF16)
    terms = jnp.concatenate([high, middle, low], axis=0)
    both = lax.dot_general(terms, terms, NT, preferred_element_type=F32)
    rows = both[0:64] + (both[64:128] + both[128:192])
    gs[0] = folded(rows[:, 0:64] + (rows[:, 64:128] + rows[:, 128:192]))
    gram_x = [remote(gs.at[0], gx.at[k - 1], x_peer(k)) for k in range(1, 4)]
    for copy in gram_x:
        copy.start()

    products(2, ya, True)
    a_one.start_second()
    products(6, yb, False)
    b_one.start_second()

    a_one.forward_first()
    for copy in gram_x:
        copy.wait_recv()
    gs[1] = gs[0] + gx[0] + gx[1] + gx[2]
    gram_y = [remote(gs.at[1], gy.at[k - 1], y_peer(k)) for k in range(1, 4)]
    for copy in gram_y:
        copy.start()
    b_one.forward_first()
    a_one.forward_second()
    b_one.forward_second()
    for copy in gram_y:
        copy.wait_recv()
    gs[2] = gs[1] + gy[0] + gy[1] + gy[2]
    gram_z = [remote(gs.at[2], gz.at[k - 1], z_peer(k)) for k in range(1, 8)]
    for copy in gram_z:
        copy.start()

    sa[:, 0] = a_one.total_first()
    sb[:, 0] = b_one.total_first()
    sa[:, 1] = a_one.total_second()
    a_two = [remote(sa.at[(y + k) % 4], ra2.at[k - 1], y_peer(k)) for k in range(1, 4)]
    for copy in a_two:
        copy.start()
    sb[:, 1] = b_one.total_second()
    b_two = [remote(sb.at[(x + k) % 4], rb2.at[k - 1], x_peer(k)) for k in range(1, 4)]
    for copy in b_two:
        copy.start()

    for copy in gram_z:
        copy.wait_recv()
    gram_sum = gs[2]
    for k in range(7):
        gram_sum = gram_sum + gz[k]
    inverse = lower_inverse(unfolded(gram_sum) * (1.0 / SAMPLES))

    def pack(z_to, halves):
        for h in range(2):
            for i in range(2):
                piece = halves[h][i * HALF : i * HALF + HALF]
                for c in range(2):
                    zp[z_to + 2 * h + i, c] = folded(piece[:, c * 64 : c * 64 + 64])

    for copy in a_two:
        copy.wait_recv()
    pack(0, [sa[y, h] + ra2[0, h] + ra2[1, h] + ra2[2, h] for h in range(2)])
    for copy in b_two:
        copy.wait_recv()
    pack(4, [sb[x, h] + rb2[0, h] + rb2[1, h] + rb2[2, h] for h in range(2)])
    last_copies = [remote(zp.at[z, 1 - core], rz.at[1, 0], twin)]
    for k in range(1, 8):
        last_copies.append(remote(zp.at[(z + k) % 8, core], rz.at[0, k], z_peer(k)))
        last_copies.append(remote(zp.at[(z + k) % 8, 1 - core], rz.at[1, k], z_other(k)))
    for copy in last_copies:
        copy.start()
    ours = pl.ds(pl.multiple_of(core * ROWS, ROWS), ROWS)
    basis[...] = jnp.dot(
        inverse,
        jnp.concatenate([skl[0, :, ours], skl[1, :, ours]], axis=0),
        precision=HIGH,
        preferred_element_type=F32,
    )
    for copy in last_copies:
        copy.wait_recv()
    own = zp[z, core]
    others = rz[1, 0]
    for k in range(1, 8):
        own = own + rz[0, k]
        others = others + rz[1, k]
    top = jnp.where(core == 0, own, others)
    bottom = jnp.where(core == 0, others, own)
    owned = jnp.concatenate([unfolded(top), unfolded(bottom)], axis=0)
    proj[...] = jnp.dot(inverse, owned, precision=HIGH, preferred_element_type=F32) * (1.0 / math.sqrt(SAMPLES))

    @pl.when(core == 0)
    def _():
        halo_near.wait_send()
        halo_far.wait_send()

    for copy in copies[1:]:
        copy.wait_send()


COPIES = 3 + 3 + 3 + 7 + 2 * 6 + 2 * 3 + 15


def shards(signal, sketch):
    return pl.pallas_call(
        kernel,
        out_shape=(
            jax.ShapeDtypeStruct((RANK, ROWS), F32),
            jax.ShapeDtypeStruct((RANK, 64), F32),
        ),
        in_specs=[pl.BlockSpec(memory_space=pl.ANY)] * 2,
        out_specs=[pl.BlockSpec(memory_space=pltpu.VMEM)] * 2,
        scratch_shapes=[
            pltpu.VMEM((HALF, LAGS * CH), BF16),
            pltpu.VMEM((2, 2240, CH), BF16),
            pltpu.VMEM((2064, CH), F32),
            pltpu.VMEM((2056, 128), F32),
            pltpu.VMEM((2052, 128), F32),
            pltpu.VMEM((2, HALF, TIMES), F32),
            pltpu.VMEM((512, DEPTH), BF16),
            pltpu.VMEM((3, 32, 128), F32),
            pltpu.VMEM((3, 32, 128), F32),
            pltpu.VMEM((3, 32, 128), F32),
            pltpu.VMEM((7, 32, 128), F32),
            pltpu.VMEM((4, 2, 4, 64, 128), F32),
            pltpu.VMEM((4, 2, 4, 64, 128), F32),
            pltpu.VMEM((2, 4, 64, 128), F32),
            pltpu.VMEM((2, 4, 64, 128), F32),
            pltpu.VMEM((2, 2, 4, 64, 128), F32),
            pltpu.VMEM((2, 2, 4, 64, 128), F32),
            pltpu.VMEM((4, 2, 64, 128), F32),
            pltpu.VMEM((4, 2, 64, 128), F32),
            pltpu.VMEM((3, 2, 64, 128), F32),
            pltpu.VMEM((3, 2, 64, 128), F32),
            pltpu.VMEM((8, 2, 16, 128), F32),
            pltpu.VMEM((2, 8, 16, 128), F32),
            pltpu.SemaphoreType.DMA((3,)),
            pltpu.SemaphoreType.DMA((COPIES,)),
            pltpu.SemaphoreType.DMA((COPIES,)),
        ],
        compiler_params=pltpu.CompilerParams(
            collective_id=0, has_side_effects=True, vmem_limit_bytes=63 * 2**20
        ),
        name="range_finder",
    )(signal, sketch)


def solution(mesh):
    in_specs = (P(("tx", "ty"), None), P())
    out_specs = (P(None, ("tx", "ty")), P(None, ("tx", "ty")))
    return jax.shard_map(shards, mesh=mesh, in_specs=in_specs, out_specs=out_specs, check_vma=False)
```

```python
import math

import jax
import jax.numpy as jnp
from jax import lax
from jax.experimental import pallas as pl
from jax.experimental.pallas import tpu as pltpu
from jax.sharding import PartitionSpec as P

MESH = pl.DeviceIdType.MESH
F32 = jnp.float32
BF16 = jnp.bfloat16
HIGH = lax.Precision.HIGHEST
NT = (((1,), (1,)), ((), ()))

ROWS = 1024
CH = 256
RANK = 64
LAGS = 64
HALF = 32
TIMES = 2048
DEPTH = 2176
SAMPLES = 262144


def lower_inverse(gram):
    row_of = lax.broadcasted_iota(jnp.int32, (8, 128), 0)
    lane_of = lax.broadcasted_iota(jnp.int32, (8, 128), 1)
    blocks = []
    for g in range(8):
        eye = jnp.where(lane_of == row_of + (64 + 8 * g), 1.0, 0.0).astype(F32)
        blocks.append(jnp.concatenate([gram[8 * g : 8 * g + 8], eye[:, 64:]], axis=1))
    for k in range(RANK - 1):
        own, at = divmod(k, 8)
        row = blocks[own][at : at + 1, :]
        scaled = row / row[:, k : k + 1]
        for g in range(own, 8):
            col = blocks[g][:, k : k + 1]
            if g == own:
                col = jnp.where(row_of[:, 0:1] > at, col, 0.0)
            blocks[g] = blocks[g] - col * scaled
    out = []
    for g in range(8):
        pivot = jnp.sum(jnp.where(lane_of == row_of + 8 * g, blocks[g], 0.0), axis=1, keepdims=True)
        out.append(blocks[g][:, 64:] * (1.0 / jnp.sqrt(pivot)))
    return jnp.concatenate(out, axis=0)


def folded(block):
    n = block.shape[0] // 2
    return jnp.concatenate([block[0:n], block[n:]], axis=1)


def unfolded(block):
    return jnp.concatenate([block[:, 0:64], block[:, 64:128]], axis=0)


class RingSum:
    def __init__(self, remote, blocks, part, place, right, left, passing, arrived):
        self.low, self.high = pl.ds(0, 2), pl.ds(2, 2)
        self.blocks, self.part, self.place, self.passing, self.arrived = blocks, part, place, passing, arrived
        self.after, self.before = (place + 1) % 4, (place + 3) % 4
        across = (place + 2) % 4
        low, high = (part, self.low), (part, self.high)
        self.across_right = remote(blocks.at[(across, *low)], passing.at[part, 0], right)
        self.across_left = remote(blocks.at[(across, *high)], passing.at[part, 1], left)
        self.after_high = remote(blocks.at[(self.after, *high)], arrived.at[(0, *high)], right)
        self.before_low = remote(blocks.at[(self.before, *low)], arrived.at[(1, *low)], left)
        self.after_low = remote(blocks.at[(self.after, *low)], arrived.at[(0, *low)], right)
        self.before_high = remote(blocks.at[(self.before, *high)], arrived.at[(1, *high)], left)

    def start(self):
        self.across_right.start()
        self.across_left.start()
        self.after_high.start()
        self.before_low.start()

    def forward(self):
        self.across_right.wait_recv()
        self.blocks[self.after, self.part, self.low] += self.passing[self.part, 0]
        self.after_low.start()
        self.across_left.wait_recv()
        self.blocks[self.before, self.part, self.high] += self.passing[self.part, 1]
        self.before_high.start()

    def total(self):
        for copy in (self.after_high, self.before_low, self.after_low, self.before_high):
            copy.wait_recv()
        return self.blocks[self.place, self.part] + self.arrived[0, self.part] + self.arrived[1, self.part]


def kernel(
    signal,
    sketch,
    basis,
    proj,
    sk_v,
    xr,
    uu,
    vv,
    vw,
    skl,
    ss,
    gs,
    gx,
    gy,
    gz,
    ya,
    yb,
    fa,
    fb,
    ra,
    rb,
    sa,
    sb,
    ra2,
    rb2,
    zp,
    rz,
    local_sem,
    send_sem,
    recv_sem,
):
    z = lax.axis_index("tx")
    ty = lax.axis_index("ty")
    y = ty // 8
    x = (ty // 2) % 4
    core = ty % 2
    me = z * 32 + ty

    def along(offset):
        index = (me + offset + 256) % 256
        return (index // 32, index % 32)

    def x_peer(k):
        return (z, y * 8 + ((x + k + 4) % 4) * 2 + core)

    def y_peer(k):
        return (z, ((y + k + 4) % 4) * 8 + x * 2 + core)

    def z_peer(k):
        return ((z + k + 8) % 8, ty)

    other = ty + 1 - 2 * core
    twin = (z, other)

    def z_other(k):
        return ((z + k + 8) % 8, other)

    copies = []

    def remote(src, dst, device):
        i = len(copies)
        copies.append(pltpu.make_async_remote_copy(
            src_ref=src,
            dst_ref=dst,
            send_sem=send_sem.at[i],
            recv_sem=recv_sem.at[i],
            device_id=device,
            device_id_type=MESH,
        ))
        return copies[i]

    own_rows = pl.ds(pl.multiple_of(core * ROWS, ROWS), ROWS)
    own_ranks = pl.ds(pl.multiple_of(core * HALF, HALF), HALF)
    get_signal = pltpu.make_async_copy(signal, xr.at[0, own_rows], local_sem.at[0])
    get_sketch = pltpu.make_async_copy(sketch.at[own_ranks], sk_v, local_sem.at[1])
    get_signal.start()
    get_sketch.start()

    barrier = pltpu.get_barrier_semaphore()
    sources = [along(2 - core), twin]
    sources += [x_peer(-k) for k in range(1, 4)]
    sources += [y_peer(-k) for k in range(1, 4)]
    sources += [z_peer(-k) for k in range(1, 8)]
    sources += [z_other(-k) for k in range(1, 8)]
    for source in sources:
        pl.semaphore_signal(barrier, inc=1, device_id=source, device_id_type=MESH)
    pl.semaphore_wait(barrier, len(sources) - 1 + 2 * (1 - core))

    halo_rows = pl.ds(TIMES, 64)
    halo_near = remote(signal.at[pl.ds(0, 64)], xr.at[0, halo_rows], along(-1))
    halo_far = pltpu.make_async_remote_copy(
        src_ref=signal.at[pl.ds(0, 64)],
        dst_ref=xr.at[0, halo_rows],
        send_sem=local_sem.at[2],
        recv_sem=recv_sem.at[0],
        device_id=along(-2),
        device_id_type=MESH,
    )

    @pl.when(core == 0)
    def _():
        halo_near.start()
        halo_far.start()

    pair_copy = remote(signal, xr.at[0, own_rows], twin)
    pair_copy.start()

    for m in range(2):
        xr[m, 2112:2240] = jnp.zeros((128, CH), BF16)
    def shifted(start, blocks, rest):
        @pl.loop(0, blocks)
        def _(i):
            at = pl.multiple_of(start + i * 128, 16)
            near = xr[0, pl.ds(at, 144)]
            xr[1, pl.ds(at, 128)] = near[8:136]

        at = pl.multiple_of(start + blocks * 128, 16)
        near = xr[0, pl.ds(at, rest + 16)]
        xr[1, pl.ds(at, rest)] = near[8 : 8 + rest]

    get_signal.wait()
    shifted(core * ROWS, 7, 112)

    get_sketch.wait()
    columns = jnp.concatenate(
        [
            jnp.concatenate([sk_v[:, (8 * q + j) * CH : (8 * q + j + 1) * CH] for q in range(8)], axis=1)
            for j in range(8)
        ],
        axis=0,
    )

    def sub_shifted(start, rows):
        moved = [xr[q % 2, pl.ds(pl.multiple_of(16 * (q // 2) + start, 16), rows)] for q in range(8)]
        uu[pl.ds(pl.multiple_of(start, 16), rows)] = lax.dot_general(
            jnp.concatenate(moved, axis=1), columns, NT, preferred_element_type=F32
        )

    sub_shifted(core * ROWS, 960)
    pair_copy.wait_recv()
    shifted(ROWS - ROWS * core - 16 * (1 - core), 7, 128)
    sub_shifted(960 - 960 * core, 1024)
    halo_near.wait_recv()

    @pl.when(me >= 254)
    def _():
        xr[0, halo_rows] = jnp.zeros((64, CH), BF16)

    near = xr[0, 2032:2128]
    xr[1, 2032:2112] = near[8:88]
    sub_shifted(1984, 80)

    vv[...] = uu[0:2056, 0:128] + uu[4:2060, 128:256]
    vw[...] = vv[0:2052] + pltpu.roll(vv[2:2054], 64, axis=1)
    group = lax.broadcasted_iota(jnp.int32, (512, 128), 1) // HALF
    merged = None
    for g in range(4):
        at = g * 512
        part = vw[at : at + 512] + pltpu.roll(vw[at + 1 : at + 513], 96, axis=1)
        merged = part if g == 0 else jnp.where(group == g, pltpu.roll(part, 32 * g, axis=1), merged)
    turned = merged.T
    for g in range(4):
        skl[core, :, g * 512 : g * 512 + 512] = turned[g * HALF : g * HALF + HALF]
    sketched_copy = remote(skl.at[core], skl.at[core], twin)
    sketched_copy.start()

    padded = jnp.concatenate([skl[core], jnp.zeros((HALF, DEPTH - TIMES), F32)], axis=1)
    for j in range(8):
        moved = padded if j == 0 else pltpu.roll(padded, j, axis=1)
        high = moved.astype(BF16)
        ss[j * HALF : j * HALF + HALF] = high
        ss[256 + j * HALF : 256 + j * HALF + HALF] = (moved - high.astype(F32)).astype(BF16)

    def products(z_to, into, x_first):
        @pl.loop(0, 2)
        def _(i):
            right = xr[i, 8 * z_to : 8 * z_to + DEPTH]
            both = jnp.dot(ss[...], right, preferred_element_type=F32)
            block = both[0:256] + both[256:512]
            at = pl.ds(pl.multiple_of(i * HALF, HALF), HALF)
            half = (z_to % 4) // 2
            for j in range(8):
                y_to = j // 2
                for x0 in range(2):
                    x_to = (j % 2) * 2 + x0
                    piece = block[j * HALF : j * HALF + HALF, x0 * 128 : x0 * 128 + 128]
                    if x_first:
                        into[x_to, half, y_to, at] = piece
                    else:
                        into[y_to, half, x_to, at] = piece

    a_one = [RingSum(remote, ya, part, x, x_peer(1), x_peer(-1), fa, ra) for part in range(2)]
    b_one = [RingSum(remote, yb, part, y, y_peer(1), y_peer(-1), fb, rb) for part in range(2)]
    products(0, ya, True)
    a_one[0].start()
    products(4, yb, False)
    b_one[0].start()

    sketched_copy.wait_recv()
    full = jnp.concatenate([skl[0], skl[1]], axis=0)
    high = full.astype(BF16)
    rest = full - high.astype(F32)
    middle = rest.astype(BF16)
    low = (rest - middle.astype(F32)).astype(BF16)
    terms = jnp.concatenate([high, middle, low], axis=0)
    both = lax.dot_general(terms, terms, NT, preferred_element_type=F32)
    rows = both[0:64] + (both[64:128] + both[128:192])
    gs[0] = folded(rows[:, 0:64] + (rows[:, 64:128] + rows[:, 128:192]))
    gram_x = [remote(gs.at[0], gx.at[k - 1], x_peer(k)) for k in range(1, 4)]
    for copy in gram_x:
        copy.start()

    products(2, ya, True)
    a_one[1].start()
    products(6, yb, False)
    b_one[1].start()

    a_one[0].forward()
    b_one[0].forward()
    for copy in gram_x:
        copy.wait_recv()
    gs[1] = gs[0] + gx[0] + gx[1] + gx[2]
    gram_y = [remote(gs.at[1], gy.at[k - 1], y_peer(k)) for k in range(1, 4)]
    for copy in gram_y:
        copy.start()
    a_one[1].forward()
    b_one[1].forward()

    def second(ring, sums, place, peer, landing):
        sums[:, ring.part] = ring.total()
        sends = [
            remote(sums.at[(place + k) % 4, ring.part], landing.at[k - 1, ring.part], peer(k)) for k in range(1, 4)
        ]
        for copy in sends:
            copy.start()
        return sends

    a_two = second(a_one[0], sa, y, y_peer, ra2)
    b_two = second(b_one[0], sb, x, x_peer, rb2)
    for copy in gram_y:
        copy.wait_recv()
    gs[2] = gs[1] + gy[0] + gy[1] + gy[2]
    gram_z = [remote(gs.at[2], gz.at[k - 1], z_peer(k)) for k in range(1, 8)]
    for copy in gram_z:
        copy.start()
    a_two += second(a_one[1], sa, y, y_peer, ra2)
    b_two += second(b_one[1], sb, x, x_peer, rb2)

    def pack(z_to, halves):
        for h in range(2):
            for i in range(2):
                piece = halves[h][i * HALF : i * HALF + HALF]
                for c in range(2):
                    zp[z_to + 2 * h + i, c] = folded(piece[:, c * 64 : c * 64 + 64])

    for copy in a_two:
        copy.wait_recv()
    pack(0, [sa[y, h] + ra2[0, h] + ra2[1, h] + ra2[2, h] for h in range(2)])
    for copy in b_two:
        copy.wait_recv()
    pack(4, [sb[x, h] + rb2[0, h] + rb2[1, h] + rb2[2, h] for h in range(2)])
    last_copies = [remote(zp.at[z, 1 - core], rz.at[1, 0], twin)]
    for k in range(1, 8):
        last_copies.append(remote(zp.at[(z + k) % 8, core], rz.at[0, k], z_peer(k)))
        last_copies.append(remote(zp.at[(z + k) % 8, 1 - core], rz.at[1, k], z_other(k)))
    for copy in last_copies:
        copy.start()

    for copy in gram_z:
        copy.wait_recv()
    gram_sum = gs[2]
    for k in range(7):
        gram_sum = gram_sum + gz[k]
    inverse = lower_inverse(unfolded(gram_sum) * (1.0 / SAMPLES))
    ours = pl.ds(pl.multiple_of(core * ROWS, ROWS), ROWS)
    basis[...] = jnp.dot(
        inverse,
        jnp.concatenate([skl[0, :, ours], skl[1, :, ours]], axis=0),
        precision=HIGH,
        preferred_element_type=F32,
    )
    for copy in last_copies:
        copy.wait_recv()
    own = zp[z, core]
    others = rz[1, 0]
    for k in range(1, 8):
        own = own + rz[0, k]
        others = others + rz[1, k]
    top = jnp.where(core == 0, own, others)
    bottom = jnp.where(core == 0, others, own)
    owned = jnp.concatenate([unfolded(top), unfolded(bottom)], axis=0)
    proj[...] = jnp.dot(inverse, owned, precision=HIGH, preferred_element_type=F32) * (1.0 / math.sqrt(SAMPLES))

    @pl.when(core == 0)
    def _():
        halo_near.wait_send()
        halo_far.wait_send()

    for copy in copies[1:]:
        copy.wait_send()


COPIES = 3 + 3 + 3 + 7 + 4 * 6 + 4 * 3 + 15


def shards(signal, sketch):
    return pl.pallas_call(
        kernel,
        out_shape=(
            jax.ShapeDtypeStruct((RANK, ROWS), F32),
            jax.ShapeDtypeStruct((RANK, 64), F32),
        ),
        in_specs=[pl.BlockSpec(memory_space=pl.ANY)] * 2,
        out_specs=[pl.BlockSpec(memory_space=pltpu.VMEM)] * 2,
        scratch_shapes=[
            pltpu.VMEM((HALF, LAGS * CH), BF16),
            pltpu.VMEM((2, 2240, CH), BF16),
            pltpu.VMEM((2064, CH), F32),
            pltpu.VMEM((2056, 128), F32),
            pltpu.VMEM((2052, 128), F32),
            pltpu.VMEM((2, HALF, TIMES), F32),
            pltpu.VMEM((512, DEPTH), BF16),
            pltpu.VMEM((3, 32, 128), F32),
            pltpu.VMEM((3, 32, 128), F32),
            pltpu.VMEM((3, 32, 128), F32),
            pltpu.VMEM((7, 32, 128), F32),
            pltpu.VMEM((4, 2, 4, 64, 128), F32),
            pltpu.VMEM((4, 2, 4, 64, 128), F32),
            pltpu.VMEM((2, 2, 2, 64, 128), F32),
            pltpu.VMEM((2, 2, 2, 64, 128), F32),
            pltpu.VMEM((2, 2, 4, 64, 128), F32),
            pltpu.VMEM((2, 2, 4, 64, 128), F32),
            pltpu.VMEM((4, 2, 64, 128), F32),
            pltpu.VMEM((4, 2, 64, 128), F32),
            pltpu.VMEM((3, 2, 64, 128), F32),
            pltpu.VMEM((3, 2, 64, 128), F32),
            pltpu.VMEM((8, 2, 16, 128), F32),
            pltpu.VMEM((2, 8, 16, 128), F32),
            pltpu.SemaphoreType.DMA((3,)),
            pltpu.SemaphoreType.DMA((COPIES,)),
            pltpu.SemaphoreType.DMA((COPIES,)),
        ],
        compiler_params=pltpu.CompilerParams(
            collective_id=0, has_side_effects=True, vmem_limit_bytes=54784 * 1024
        ),
        name="range_finder",
    )(signal, sketch)


def solution(mesh):
    in_specs = (P(("tx", "ty"), None), P())
    out_specs = (P(None, ("tx", "ty")), P(None, ("tx", "ty")))
    return jax.shard_map(shards, mesh=mesh, in_specs=in_specs, out_specs=out_specs, check_vma=False)
```

```python
import math

import jax
import jax.numpy as jnp
from jax import lax
from jax.experimental import pallas as pl
from jax.experimental.pallas import tpu as pltpu
from jax.sharding import PartitionSpec as P

MESH = pl.DeviceIdType.MESH
F32 = jnp.float32
BF16 = jnp.bfloat16
HIGH = lax.Precision.HIGHEST
NT = (((1,), (1,)), ((), ()))

ROWS = 1024
CH = 256
RANK = 64
LAGS = 64
HALF = 32
TIMES = 2048
DEPTH = 2176
SAMPLES = 262144


def lower_inverse(gram):
    row_of = lax.broadcasted_iota(jnp.int32, (8, 128), 0)
    lane_of = lax.broadcasted_iota(jnp.int32, (8, 128), 1)
    blocks = []
    for g in range(8):
        eye = jnp.where(lane_of == row_of + (64 + 8 * g), 1.0, 0.0).astype(F32)
        blocks.append(jnp.concatenate([gram[8 * g : 8 * g + 8], eye[:, 64:]], axis=1))
    for k in range(RANK - 1):
        own, at = divmod(k, 8)
        row = blocks[own][at : at + 1, :]
        scaled = row / row[:, k : k + 1]
        for g in range(own, 8):
            col = blocks[g][:, k : k + 1]
            if g == own:
                col = jnp.where(row_of[:, 0:1] > at, col, 0.0)
            blocks[g] = blocks[g] - col * scaled
    out = []
    for g in range(8):
        pivot = jnp.sum(jnp.where(lane_of == row_of + 8 * g, blocks[g], 0.0), axis=1, keepdims=True)
        out.append(blocks[g][:, 64:] * (1.0 / jnp.sqrt(pivot)))
    return jnp.concatenate(out, axis=0)


def folded(block):
    n = block.shape[0] // 2
    return jnp.concatenate([block[0:n], block[n:]], axis=1)


def unfolded(block):
    return jnp.concatenate([block[:, 0:64], block[:, 64:128]], axis=0)


class RingSum:
    def __init__(self, remote, blocks, part, place, right, left, passing, arrived):
        self.low, self.high = pl.ds(0, 2), pl.ds(2, 2)
        self.blocks, self.part, self.place, self.passing, self.arrived = blocks, part, place, passing, arrived
        self.after, self.before = (place + 1) % 4, (place + 3) % 4
        across = (place + 2) % 4
        low, high = (part, self.low), (part, self.high)
        self.across_right = remote(blocks.at[(across, *low)], passing.at[part, 0], right)
        self.across_left = remote(blocks.at[(across, *high)], passing.at[part, 1], left)
        self.after_high = remote(blocks.at[(self.after, *high)], arrived.at[(0, *high)], right)
        self.before_low = remote(blocks.at[(self.before, *low)], arrived.at[(1, *low)], left)
        self.after_low = remote(blocks.at[(self.after, *low)], arrived.at[(0, *low)], right)
        self.before_high = remote(blocks.at[(self.before, *high)], arrived.at[(1, *high)], left)

    def start(self):
        self.across_right.start()
        self.across_left.start()
        self.after_high.start()
        self.before_low.start()

    def forward(self):
        self.across_right.wait_recv()
        self.blocks[self.after, self.part, self.low] += self.passing[self.part, 0]
        self.after_low.start()
        self.across_left.wait_recv()
        self.blocks[self.before, self.part, self.high] += self.passing[self.part, 1]
        self.before_high.start()

    def total(self):
        for copy in (self.after_high, self.before_low, self.after_low, self.before_high):
            copy.wait_recv()
        return self.blocks[self.place, self.part] + self.arrived[0, self.part] + self.arrived[1, self.part]


def kernel(
    signal,
    sketch,
    basis,
    proj,
    sk_v,
    xr,
    uu,
    vv,
    vw,
    skl,
    ss,
    gs,
    gx,
    gy,
    gz,
    ya,
    yb,
    fa,
    fb,
    ra,
    rb,
    sa,
    sb,
    ra2,
    rb2,
    zp,
    rz,
    local_sem,
    send_sem,
    recv_sem,
    last_send,
    last_recv,
):
    z = lax.axis_index("tx")
    ty = lax.axis_index("ty")
    y = ty // 8
    x = (ty // 2) % 4
    core = ty % 2
    me = z * 32 + ty

    def along(offset):
        index = (me + offset + 256) % 256
        return (index // 32, index % 32)

    def x_peer(k):
        return (z, y * 8 + ((x + k + 4) % 4) * 2 + core)

    def y_peer(k):
        return (z, ((y + k + 4) % 4) * 8 + x * 2 + core)

    def z_peer(k):
        return ((z + k + 8) % 8, ty)

    other = ty + 1 - 2 * core
    twin = (z, other)

    def z_other(k):
        return ((z + k + 8) % 8, other)

    copies = []

    def remote(src, dst, device):
        i = len(copies)
        copies.append(pltpu.make_async_remote_copy(
            src_ref=src,
            dst_ref=dst,
            send_sem=send_sem.at[i],
            recv_sem=recv_sem.at[i],
            device_id=device,
            device_id_type=MESH,
        ))
        return copies[i]

    own_rows = pl.ds(pl.multiple_of(core * ROWS, ROWS), ROWS)
    own_ranks = pl.ds(pl.multiple_of(core * HALF, HALF), HALF)
    get_signal = pltpu.make_async_copy(signal, xr.at[0, own_rows], local_sem.at[0])
    get_sketch = pltpu.make_async_copy(sketch.at[own_ranks], sk_v, local_sem.at[1])
    get_signal.start()
    get_sketch.start()

    barrier = pltpu.get_barrier_semaphore()
    sources = [along(2 - core), twin]
    sources += [x_peer(-k) for k in range(1, 4)]
    sources += [y_peer(-k) for k in range(1, 4)]
    sources += [z_peer(-k) for k in range(1, 8)]
    sources += [z_other(-k) for k in range(1, 8)]
    for source in sources:
        pl.semaphore_signal(barrier, inc=1, device_id=source, device_id_type=MESH)
    pl.semaphore_wait(barrier, len(sources) - 1 + 2 * (1 - core))

    halo_rows = pl.ds(TIMES, 64)
    halo_near = remote(signal.at[pl.ds(0, 64)], xr.at[0, halo_rows], along(-1))
    halo_far = pltpu.make_async_remote_copy(
        src_ref=signal.at[pl.ds(0, 64)],
        dst_ref=xr.at[0, halo_rows],
        send_sem=local_sem.at[2],
        recv_sem=recv_sem.at[0],
        device_id=along(-2),
        device_id_type=MESH,
    )

    @pl.when(core == 0)
    def _():
        halo_near.start()
        halo_far.start()

    pair_copy = remote(signal, xr.at[0, own_rows], twin)
    pair_copy.start()

    for m in range(2):
        xr[m, 2112:2240] = jnp.zeros((128, CH), BF16)
    def shifted(start, blocks, rest):
        @pl.loop(0, blocks)
        def _(i):
            at = pl.multiple_of(start + i * 128, 16)
            near = xr[0, pl.ds(at, 144)]
            xr[1, pl.ds(at, 128)] = near[8:136]

        at = pl.multiple_of(start + blocks * 128, 16)
        near = xr[0, pl.ds(at, rest + 16)]
        xr[1, pl.ds(at, rest)] = near[8 : 8 + rest]

    get_signal.wait()
    shifted(core * ROWS, 7, 112)

    get_sketch.wait()
    columns = jnp.concatenate(
        [
            jnp.concatenate([sk_v[:, (8 * q + j) * CH : (8 * q + j + 1) * CH] for q in range(8)], axis=1)
            for j in range(8)
        ],
        axis=0,
    )

    def sub_shifted(start, rows):
        moved = [xr[q % 2, pl.ds(pl.multiple_of(16 * (q // 2) + start, 16), rows)] for q in range(8)]
        uu[pl.ds(pl.multiple_of(start, 16), rows)] = lax.dot_general(
            jnp.concatenate(moved, axis=1), columns, NT, preferred_element_type=F32
        )

    sub_shifted(core * ROWS, 960)
    pair_copy.wait_recv()
    shifted(ROWS - ROWS * core - 16 * (1 - core), 7, 128)
    sub_shifted(960 - 960 * core, 1024)
    halo_near.wait_recv()

    @pl.when(me >= 254)
    def _():
        xr[0, halo_rows] = jnp.zeros((64, CH), BF16)

    near = xr[0, 2032:2128]
    xr[1, 2032:2112] = near[8:88]
    sub_shifted(1984, 80)

    vv[...] = uu[0:2056, 0:128] + uu[4:2060, 128:256]
    vw[...] = vv[0:2052] + pltpu.roll(vv[2:2054], 64, axis=1)
    group = lax.broadcasted_iota(jnp.int32, (512, 128), 1) // HALF
    merged = None
    for g in range(4):
        at = g * 512
        part = vw[at : at + 512] + pltpu.roll(vw[at + 1 : at + 513], 96, axis=1)
        merged = part if g == 0 else jnp.where(group == g, pltpu.roll(part, 32 * g, axis=1), merged)
    turned = merged.T
    for g in range(4):
        skl[core, :, g * 512 : g * 512 + 512] = turned[g * HALF : g * HALF + HALF]
    sketched_copy = remote(skl.at[core], skl.at[core], twin)
    sketched_copy.start()

    padded = jnp.concatenate([skl[core], jnp.zeros((HALF, DEPTH - TIMES), F32)], axis=1)
    for j in range(8):
        moved = padded if j == 0 else pltpu.roll(padded, j, axis=1)
        high = moved.astype(BF16)
        ss[j * HALF : j * HALF + HALF] = high
        ss[256 + j * HALF : 256 + j * HALF + HALF] = (moved - high.astype(F32)).astype(BF16)

    def products(z_to, into, x_first):
        @pl.loop(0, 2)
        def _(i):
            right = xr[i, 8 * z_to : 8 * z_to + DEPTH]
            both = jnp.dot(ss[...], right, preferred_element_type=F32)
            block = both[0:256] + both[256:512]
            at = pl.ds(pl.multiple_of(i * HALF, HALF), HALF)
            half = (z_to % 4) // 2
            for j in range(8):
                y_to = j // 2
                for x0 in range(2):
                    x_to = (j % 2) * 2 + x0
                    piece = block[j * HALF : j * HALF + HALF, x0 * 128 : x0 * 128 + 128]
                    if x_first:
                        into[x_to, half, y_to, at] = piece
                    else:
                        into[y_to, half, x_to, at] = piece

    a_one = [RingSum(remote, ya, part, x, x_peer(1), x_peer(-1), fa, ra) for part in range(2)]
    b_one = [RingSum(remote, yb, part, y, y_peer(1), y_peer(-1), fb, rb) for part in range(2)]
    products(0, ya, True)
    a_one[0].start()
    products(4, yb, False)
    b_one[0].start()

    products(2, ya, True)
    a_one[1].start()
    products(6, yb, False)
    b_one[1].start()

    sketched_copy.wait_recv()
    full = jnp.concatenate([skl[0], skl[1]], axis=0)
    high = full.astype(BF16)
    rest = full - high.astype(F32)
    middle = rest.astype(BF16)
    low = (rest - middle.astype(F32)).astype(BF16)
    terms = jnp.concatenate([high, middle, low], axis=0)
    both = lax.dot_general(terms, terms, NT, preferred_element_type=F32)
    rows = both[0:64] + (both[64:128] + both[128:192])
    gs[0] = folded(rows[:, 0:64] + (rows[:, 64:128] + rows[:, 128:192]))
    gram_x = [remote(gs.at[0], gx.at[k - 1], x_peer(k)) for k in range(1, 4)]
    for copy in gram_x:
        copy.start()

    a_one[0].forward()
    b_one[0].forward()
    for copy in gram_x:
        copy.wait_recv()
    gs[1] = gs[0] + gx[0] + gx[1] + gx[2]
    gram_y = [remote(gs.at[1], gy.at[k - 1], y_peer(k)) for k in range(1, 4)]
    for copy in gram_y:
        copy.start()
    a_one[1].forward()
    b_one[1].forward()

    def second(ring, sums, place, peer, landing):
        sums[:, ring.part] = ring.total()
        sends = [
            remote(sums.at[(place + k) % 4, ring.part], landing.at[k - 1, ring.part], peer(k)) for k in range(1, 4)
        ]
        for copy in sends:
            copy.start()
        return sends

    a_two = second(a_one[0], sa, y, y_peer, ra2)
    b_two = second(b_one[0], sb, x, x_peer, rb2)
    for copy in gram_y:
        copy.wait_recv()
    gs[2] = gs[1] + gy[0] + gy[1] + gy[2]
    gram_z = [remote(gs.at[2], gz.at[k - 1], z_peer(k)) for k in range(1, 8)]
    for copy in gram_z:
        copy.start()
    a_two += second(a_one[1], sa, y, y_peer, ra2)
    b_two += second(b_one[1], sb, x, x_peer, rb2)

    def pack(z_to, halves):
        for h in range(2):
            for i in range(2):
                piece = halves[h][i * HALF : i * HALF + HALF]
                for c in range(2):
                    zp[z_to + 2 * h + i, c] = folded(piece[:, c * 64 : c * 64 + 64])

    def along_z(z_to):
        k = (z_to - z + 8) % 8
        pair = []
        for which, device in ((0, (z_to, ty)), (1, (z_to, other))):
            pair.append(pltpu.make_async_remote_copy(
                src_ref=zp.at[z_to, (core + which) % 2],
                dst_ref=rz.at[which, k],
                send_sem=last_send.at[which, k],
                recv_sem=last_recv.at[which, k],
                device_id=device,
                device_id_type=MESH,
            ))
        return pair

    def send_along_z(first):
        for z_to in range(first, first + 4):
            same_core, other_core = along_z(z_to)

            @pl.when(z != z_to)
            def _():
                same_core.start()

            other_core.start()

    for copy in a_two:
        copy.wait_recv()
    pack(0, [sa[y, h] + ra2[0, h] + ra2[1, h] + ra2[2, h] for h in range(2)])
    send_along_z(0)
    for copy in b_two:
        copy.wait_recv()
    pack(4, [sb[x, h] + rb2[0, h] + rb2[1, h] + rb2[2, h] for h in range(2)])
    send_along_z(4)

    for copy in gram_z:
        copy.wait_recv()
    gram_sum = gs[2]
    for k in range(7):
        gram_sum = gram_sum + gz[k]
    inverse = lower_inverse(unfolded(gram_sum) * (1.0 / SAMPLES))
    ours = pl.ds(pl.multiple_of(core * ROWS, ROWS), ROWS)
    basis[...] = jnp.dot(
        inverse,
        jnp.concatenate([skl[0, :, ours], skl[1, :, ours]], axis=0),
        precision=HIGH,
        preferred_element_type=F32,
    )
    landed = [along_z((z + k) % 8) for k in range(8)]
    for k in range(8):
        if k > 0:
            landed[k][0].wait_recv()
        landed[k][1].wait_recv()
    own = zp[z, core]
    others = rz[1, 0]
    for k in range(1, 8):
        own = own + rz[0, k]
        others = others + rz[1, k]
    top = jnp.where(core == 0, own, others)
    bottom = jnp.where(core == 0, others, own)
    owned = jnp.concatenate([unfolded(top), unfolded(bottom)], axis=0)
    proj[...] = jnp.dot(inverse, owned, precision=HIGH, preferred_element_type=F32) * (1.0 / math.sqrt(SAMPLES))

    @pl.when(core == 0)
    def _():
        halo_near.wait_send()
        halo_far.wait_send()

    for copy in copies[1:]:
        copy.wait_send()
    for k in range(8):
        if k > 0:
            landed[k][0].wait_send()
        landed[k][1].wait_send()


COPIES = 3 + 3 + 3 + 7 + 4 * 6 + 4 * 3


def shards(signal, sketch):
    return pl.pallas_call(
        kernel,
        out_shape=(
            jax.ShapeDtypeStruct((RANK, ROWS), F32),
            jax.ShapeDtypeStruct((RANK, 64), F32),
        ),
        in_specs=[pl.BlockSpec(memory_space=pl.ANY)] * 2,
        out_specs=[pl.BlockSpec(memory_space=pltpu.VMEM)] * 2,
        scratch_shapes=[
            pltpu.VMEM((HALF, LAGS * CH), BF16),
            pltpu.VMEM((2, 2240, CH), BF16),
            pltpu.VMEM((2064, CH), F32),
            pltpu.VMEM((2056, 128), F32),
            pltpu.VMEM((2052, 128), F32),
            pltpu.VMEM((2, HALF, TIMES), F32),
            pltpu.VMEM((512, DEPTH), BF16),
            pltpu.VMEM((3, 32, 128), F32),
            pltpu.VMEM((3, 32, 128), F32),
            pltpu.VMEM((3, 32, 128), F32),
            pltpu.VMEM((7, 32, 128), F32),
            pltpu.VMEM((4, 2, 4, 64, 128), F32),
            pltpu.VMEM((4, 2, 4, 64, 128), F32),
            pltpu.VMEM((2, 2, 2, 64, 128), F32),
            pltpu.VMEM((2, 2, 2, 64, 128), F32),
            pltpu.VMEM((2, 2, 4, 64, 128), F32),
            pltpu.VMEM((2, 2, 4, 64, 128), F32),
            pltpu.VMEM((4, 2, 64, 128), F32),
            pltpu.VMEM((4, 2, 64, 128), F32),
            pltpu.VMEM((3, 2, 64, 128), F32),
            pltpu.VMEM((3, 2, 64, 128), F32),
            pltpu.VMEM((8, 2, 16, 128), F32),
            pltpu.VMEM((2, 8, 16, 128), F32),
            pltpu.SemaphoreType.DMA((3,)),
            pltpu.SemaphoreType.DMA((COPIES,)),
            pltpu.SemaphoreType.DMA((COPIES,)),
            pltpu.SemaphoreType.DMA((2, 8)),
            pltpu.SemaphoreType.DMA((2, 8)),
        ],
        compiler_params=pltpu.CompilerParams(
            collective_id=0, has_side_effects=True, vmem_limit_bytes=54784 * 1024
        ),
        name="range_finder",
    )(signal, sketch)


def solution(mesh):
    in_specs = (P(("tx", "ty"), None), P())
    out_specs = (P(None, ("tx", "ty")), P(None, ("tx", "ty")))
    return jax.shard_map(shards, mesh=mesh, in_specs=in_specs, out_specs=out_specs, check_vma=False)
```

```python
import math

import jax
import jax.numpy as jnp
from jax import lax
from jax.experimental import pallas as pl
from jax.experimental.pallas import tpu as pltpu
from jax.sharding import PartitionSpec as P

MESH = pl.DeviceIdType.MESH
F32 = jnp.float32
BF16 = jnp.bfloat16
HIGH = lax.Precision.HIGHEST
NT = (((1,), (1,)), ((), ()))

ROWS = 1024
CH = 256
RANK = 64
LAGS = 64
HALF = 32
TIMES = 2048
DEPTH = 2176
SAMPLES = 262144


def lower_inverse(gram):
    row_of = lax.broadcasted_iota(jnp.int32, (8, 128), 0)
    lane_of = lax.broadcasted_iota(jnp.int32, (8, 128), 1)
    blocks = []
    for g in range(8):
        eye = jnp.where(lane_of == row_of + (64 + 8 * g), 1.0, 0.0).astype(F32)
        blocks.append(jnp.concatenate([gram[8 * g : 8 * g + 8], eye[:, 64:]], axis=1))
    for k in range(RANK - 1):
        own, at = divmod(k, 8)
        row = blocks[own][at : at + 1, :]
        scaled = row / row[:, k : k + 1]
        for g in range(own, 8):
            col = blocks[g][:, k : k + 1]
            if g == own:
                col = jnp.where(row_of[:, 0:1] > at, col, 0.0)
            blocks[g] = blocks[g] - col * scaled
    out = []
    for g in range(8):
        pivot = jnp.sum(jnp.where(lane_of == row_of + 8 * g, blocks[g], 0.0), axis=1, keepdims=True)
        out.append(blocks[g][:, 64:] * (1.0 / jnp.sqrt(pivot)))
    return jnp.concatenate(out, axis=0)


def folded(block):
    n = block.shape[0] // 2
    return jnp.concatenate([block[0:n], block[n:]], axis=1)


def unfolded(block):
    return jnp.concatenate([block[:, 0:64], block[:, 64:128]], axis=0)


class RingSum:
    def __init__(self, remote, blocks, part, place, right, left, passing, arrived):
        self.blocks, self.part, self.place, self.passing, self.arrived = blocks, part, place, passing, arrived
        forward, backward = (left, right) if part else (right, left)
        self.ahead, behind = (place + (3 if part else 1)) % 4, (place + (1 if part else 3)) % 4
        self.across = remote(blocks.at[(place + 2) % 4, part], passing.at[part], forward)
        self.back = remote(blocks.at[behind, part], arrived.at[1, part], backward)
        self.on = remote(blocks.at[self.ahead, part], arrived.at[0, part], forward)

    def start(self):
        self.across.start()
        self.back.start()

    def forward(self):
        self.across.wait_recv()
        self.blocks[self.ahead, self.part] += self.passing[self.part]
        self.on.start()

    def total(self):
        self.back.wait_recv()
        self.on.wait_recv()
        return self.blocks[self.place, self.part] + self.arrived[0, self.part] + self.arrived[1, self.part]


def kernel(
    signal,
    sketch,
    basis,
    proj,
    sk_v,
    xr,
    uu,
    vv,
    vw,
    skl,
    ss,
    gs,
    gx,
    gy,
    gz,
    ya,
    yb,
    fa,
    fb,
    ra,
    rb,
    sa,
    sb,
    ra2,
    rb2,
    zp,
    rz,
    local_sem,
    send_sem,
    recv_sem,
    last_send,
    last_recv,
):
    z = lax.axis_index("tx")
    ty = lax.axis_index("ty")
    y = ty // 8
    x = (ty // 2) % 4
    core = ty % 2
    me = z * 32 + ty

    def along(offset):
        index = (me + offset + 256) % 256
        return (index // 32, index % 32)

    def x_peer(k):
        return (z, y * 8 + ((x + k + 4) % 4) * 2 + core)

    def y_peer(k):
        return (z, ((y + k + 4) % 4) * 8 + x * 2 + core)

    def z_peer(k):
        return ((z + k + 8) % 8, ty)

    other = ty + 1 - 2 * core
    twin = (z, other)

    def z_other(k):
        return ((z + k + 8) % 8, other)

    copies = []

    def remote(src, dst, device):
        i = len(copies)
        copies.append(pltpu.make_async_remote_copy(
            src_ref=src,
            dst_ref=dst,
            send_sem=send_sem.at[i],
            recv_sem=recv_sem.at[i],
            device_id=device,
            device_id_type=MESH,
        ))
        return copies[i]

    own_rows = pl.ds(pl.multiple_of(core * ROWS, ROWS), ROWS)
    own_ranks = pl.ds(pl.multiple_of(core * HALF, HALF), HALF)
    get_signal = pltpu.make_async_copy(signal, xr.at[0, own_rows], local_sem.at[0])
    get_sketch = pltpu.make_async_copy(sketch.at[own_ranks], sk_v, local_sem.at[1])
    get_signal.start()
    get_sketch.start()

    barrier = pltpu.get_barrier_semaphore()
    sources = [along(2 - core), twin]
    sources += [x_peer(-k) for k in range(1, 4)]
    sources += [y_peer(-k) for k in range(1, 4)]
    sources += [z_peer(-k) for k in range(1, 8)]
    sources += [z_other(-k) for k in range(1, 8)]
    for source in sources:
        pl.semaphore_signal(barrier, inc=1, device_id=source, device_id_type=MESH)
    pl.semaphore_wait(barrier, len(sources) - 1 + 2 * (1 - core))

    halo_rows = pl.ds(TIMES, 64)
    halo_near = remote(signal.at[pl.ds(0, 64)], xr.at[0, halo_rows], along(-1))
    halo_far = pltpu.make_async_remote_copy(
        src_ref=signal.at[pl.ds(0, 64)],
        dst_ref=xr.at[0, halo_rows],
        send_sem=local_sem.at[2],
        recv_sem=recv_sem.at[0],
        device_id=along(-2),
        device_id_type=MESH,
    )

    @pl.when(core == 0)
    def _():
        halo_near.start()
        halo_far.start()

    pair_copy = remote(signal, xr.at[0, own_rows], twin)
    pair_copy.start()

    for m in range(2):
        xr[m, 2112:2240] = jnp.zeros((128, CH), BF16)
    def shifted(start, blocks, rest):
        for i in range(blocks):
            at = pl.multiple_of(start + i * 128, 16)
            near = xr[0, pl.ds(at, 144)]
            xr[1, pl.ds(at, 128)] = near[8:136]

        at = pl.multiple_of(start + blocks * 128, 16)
        near = xr[0, pl.ds(at, rest + 16)]
        xr[1, pl.ds(at, rest)] = near[8 : 8 + rest]

    get_signal.wait()
    shifted(core * ROWS, 7, 112)

    get_sketch.wait()
    columns = jnp.concatenate(
        [
            jnp.concatenate([sk_v[:, (8 * q + j) * CH : (8 * q + j + 1) * CH] for q in range(8)], axis=1)
            for j in range(8)
        ],
        axis=0,
    )

    def sub_shifted(start, rows):
        moved = [xr[q % 2, pl.ds(pl.multiple_of(16 * (q // 2) + start, 16), rows)] for q in range(8)]
        uu[pl.ds(pl.multiple_of(start, 16), rows)] = lax.dot_general(
            jnp.concatenate(moved, axis=1), columns, NT, preferred_element_type=F32
        )

    sub_shifted(core * ROWS, 960)
    pair_copy.wait_recv()
    shifted(ROWS - ROWS * core - 16 * (1 - core), 7, 128)
    sub_shifted(960 - 960 * core, 1024)
    halo_near.wait_recv()

    @pl.when(me >= 254)
    def _():
        xr[0, halo_rows] = jnp.zeros((64, CH), BF16)

    near = xr[0, 2032:2128]
    xr[1, 2032:2112] = near[8:88]
    sub_shifted(1984, 80)

    vv[...] = uu[0:2056, 0:128] + uu[4:2060, 128:256]
    vw[...] = vv[0:2052] + pltpu.roll(vv[2:2054], 64, axis=1)
    group = lax.broadcasted_iota(jnp.int32, (512, 128), 1) // HALF
    merged = None
    for g in range(4):
        at = g * 512
        part = vw[at : at + 512] + pltpu.roll(vw[at + 1 : at + 513], 96, axis=1)
        merged = part if g == 0 else jnp.where(group == g, pltpu.roll(part, 32 * g, axis=1), merged)
    turned = merged.T
    for g in range(4):
        skl[core, :, g * 512 : g * 512 + 512] = turned[g * HALF : g * HALF + HALF]
    sketched_copy = remote(skl.at[core], skl.at[core], twin)
    sketched_copy.start()

    padded = jnp.concatenate([skl[core], jnp.zeros((HALF, DEPTH - TIMES), F32)], axis=1)
    for j in range(8):
        moved = padded if j == 0 else pltpu.roll(padded, j, axis=1)
        high = moved.astype(BF16)
        ss[j * HALF : j * HALF + HALF] = high
        ss[256 + j * HALF : 256 + j * HALF + HALF] = (moved - high.astype(F32)).astype(BF16)

    def products(z_to, into, x_first):
        for i in range(2):
            right = xr[i, 8 * z_to : 8 * z_to + DEPTH]
            both = jnp.dot(ss[...], right, preferred_element_type=F32)
            block = both[0:256] + both[256:512]
            at = slice(i * HALF, i * HALF + HALF)
            half = (z_to % 4) // 2
            for j in range(8):
                y_to = j // 2
                for x0 in range(2):
                    x_to = (j % 2) * 2 + x0
                    piece = block[j * HALF : j * HALF + HALF, x0 * 128 : x0 * 128 + 128]
                    if x_first:
                        into[x_to, half, y_to, at] = piece
                    else:
                        into[y_to, half, x_to, at] = piece

    a_one = [RingSum(remote, ya, part, x, x_peer(1), x_peer(-1), fa, ra) for part in range(2)]
    b_one = [RingSum(remote, yb, part, y, y_peer(1), y_peer(-1), fb, rb) for part in range(2)]
    products(0, ya, True)
    a_one[0].start()
    products(4, yb, False)
    b_one[0].start()

    products(2, ya, True)
    a_one[1].start()
    products(6, yb, False)
    b_one[1].start()

    sketched_copy.wait_recv()
    full = jnp.concatenate([skl[0], skl[1]], axis=0)
    high = full.astype(BF16)
    rest = full - high.astype(F32)
    middle = rest.astype(BF16)
    low = (rest - middle.astype(F32)).astype(BF16)
    terms = jnp.concatenate([high, middle, low], axis=0)
    both = lax.dot_general(terms, terms, NT, preferred_element_type=F32)
    rows = both[0:64] + (both[64:128] + both[128:192])
    gs[0] = folded(rows[:, 0:64] + (rows[:, 64:128] + rows[:, 128:192]))
    gram_x = [remote(gs.at[0], gx.at[k - 1], x_peer(k)) for k in range(1, 4)]
    for copy in gram_x:
        copy.start()

    a_one[0].forward()
    b_one[0].forward()
    for copy in gram_x:
        copy.wait_recv()
    gs[1] = gs[0] + gx[0] + gx[1] + gx[2]
    gram_y = [remote(gs.at[1], gy.at[k - 1], y_peer(k)) for k in range(1, 4)]
    for copy in gram_y:
        copy.start()
    a_one[1].forward()
    b_one[1].forward()

    def second(rings, sums, place, peer, landing):
        for ring in rings:
            sums[:, ring.part] = ring.total()
        sends = [remote(sums.at[(place + k) % 4], landing.at[k - 1], peer(k)) for k in (2, 1, 3)]
        for copy in sends:
            copy.start()
        return sends

    for copy in gram_y:
        copy.wait_recv()
    gs[2] = gs[1] + gy[0] + gy[1] + gy[2]
    gram_z = [remote(gs.at[2], gz.at[k - 1], z_peer(k)) for k in range(1, 8)]
    for copy in gram_z:
        copy.start()
    a_two = second(a_one, sa, y, y_peer, ra2)
    b_two = second(b_one, sb, x, x_peer, rb2)

    def pack(z_to, halves):
        for h in range(2):
            for i in range(2):
                piece = halves[h][i * HALF : i * HALF + HALF]
                for c in range(2):
                    zp[z_to + 2 * h + i, c] = folded(piece[:, c * 64 : c * 64 + 64])

    def along_z(z_to):
        k = (z_to - z + 8) % 8
        pair = []
        for which, device in ((0, (z_to, ty)), (1, (z_to, other))):
            pair.append(pltpu.make_async_remote_copy(
                src_ref=zp.at[z_to, (core + which) % 2],
                dst_ref=rz.at[which, k],
                send_sem=last_send.at[which, k],
                recv_sem=last_recv.at[which, k],
                device_id=device,
                device_id_type=MESH,
            ))
        return pair

    def send_along_z(first):
        for z_to in range(first, first + 4):
            same_core, other_core = along_z(z_to)

            @pl.when(z != z_to)
            def _():
                same_core.start()

            other_core.start()

    for copy in a_two:
        copy.wait_recv()
    pack(0, [sa[y, h] + ra2[0, h] + ra2[1, h] + ra2[2, h] for h in range(2)])
    send_along_z(0)
    for copy in b_two:
        copy.wait_recv()
    pack(4, [sb[x, h] + rb2[0, h] + rb2[1, h] + rb2[2, h] for h in range(2)])
    send_along_z(4)

    for copy in gram_z:
        copy.wait_recv()
    gram_sum = gs[2]
    for k in range(7):
        gram_sum = gram_sum + gz[k]
    inverse = lower_inverse(unfolded(gram_sum) * (1.0 / SAMPLES))
    ours = pl.ds(pl.multiple_of(core * ROWS, ROWS), ROWS)
    basis[...] = jnp.dot(
        inverse,
        jnp.concatenate([skl[0, :, ours], skl[1, :, ours]], axis=0),
        precision=HIGH,
        preferred_element_type=F32,
    )
    landed = [along_z((z + k) % 8) for k in range(8)]
    for k in range(8):
        if k > 0:
            landed[k][0].wait_recv()
        landed[k][1].wait_recv()
    own = zp[z, core]
    others = rz[1, 0]
    for k in range(1, 8):
        own = own + rz[0, k]
        others = others + rz[1, k]
    top = jnp.where(core == 0, own, others)
    bottom = jnp.where(core == 0, others, own)
    owned = jnp.concatenate([unfolded(top), unfolded(bottom)], axis=0)
    proj[...] = jnp.dot(inverse, owned, precision=HIGH, preferred_element_type=F32) * (1.0 / math.sqrt(SAMPLES))

    @pl.when(core == 0)
    def _():
        halo_near.wait_send()
        halo_far.wait_send()

    for copy in copies[1:]:
        copy.wait_send()
    for k in range(8):
        if k > 0:
            landed[k][0].wait_send()
        landed[k][1].wait_send()


COPIES = 3 + 3 + 3 + 7 + 4 * 3 + 2 * 3


def shards(signal, sketch):
    return pl.pallas_call(
        kernel,
        out_shape=(
            jax.ShapeDtypeStruct((RANK, ROWS), F32),
            jax.ShapeDtypeStruct((RANK, 64), F32),
        ),
        in_specs=[pl.BlockSpec(memory_space=pl.ANY)] * 2,
        out_specs=[pl.BlockSpec(memory_space=pltpu.VMEM)] * 2,
        scratch_shapes=[
            pltpu.VMEM((HALF, LAGS * CH), BF16),
            pltpu.VMEM((2, 2240, CH), BF16),
            pltpu.VMEM((2064, CH), F32),
            pltpu.VMEM((2056, 128), F32),
            pltpu.VMEM((2052, 128), F32),
            pltpu.VMEM((2, HALF, TIMES), F32),
            pltpu.VMEM((512, DEPTH), BF16),
            pltpu.VMEM((3, 32, 128), F32),
            pltpu.VMEM((3, 32, 128), F32),
            pltpu.VMEM((3, 32, 128), F32),
            pltpu.VMEM((7, 32, 128), F32),
            pltpu.VMEM((4, 2, 4, 64, 128), F32),
            pltpu.VMEM((4, 2, 4, 64, 128), F32),
            pltpu.VMEM((2, 4, 64, 128), F32),
            pltpu.VMEM((2, 4, 64, 128), F32),
            pltpu.VMEM((2, 2, 4, 64, 128), F32),
            pltpu.VMEM((2, 2, 4, 64, 128), F32),
            pltpu.VMEM((4, 2, 64, 128), F32),
            pltpu.VMEM((4, 2, 64, 128), F32),
            pltpu.VMEM((3, 2, 64, 128), F32),
            pltpu.VMEM((3, 2, 64, 128), F32),
            pltpu.VMEM((8, 2, 16, 128), F32),
            pltpu.VMEM((2, 8, 16, 128), F32),
            pltpu.SemaphoreType.DMA((3,)),
            pltpu.SemaphoreType.DMA((COPIES,)),
            pltpu.SemaphoreType.DMA((COPIES,)),
            pltpu.SemaphoreType.DMA((2, 8)),
            pltpu.SemaphoreType.DMA((2, 8)),
        ],
        compiler_params=pltpu.CompilerParams(
            collective_id=0, has_side_effects=True, vmem_limit_bytes=54784 * 1024
        ),
        name="range_finder",
    )(signal, sketch)


def solution(mesh):
    in_specs = (P(("tx", "ty"), None), P())
    out_specs = (P(None, ("tx", "ty")), P(None, ("tx", "ty")))
    return jax.shard_map(shards, mesh=mesh, in_specs=in_specs, out_specs=out_specs, check_vma=False)
```

```python
import math

import jax
import jax.numpy as jnp
from jax import lax
from jax.experimental import pallas as pl
from jax.experimental.pallas import tpu as pltpu
from jax.sharding import PartitionSpec as P

MESH = pl.DeviceIdType.MESH
F32 = jnp.float32
BF16 = jnp.bfloat16
HIGH = lax.Precision.HIGHEST
NT = (((1,), (1,)), ((), ()))

ROWS = 1024
CH = 256
RANK = 64
LAGS = 64
HALF = 32
TIMES = 2048
DEPTH = 2176
SAMPLES = 262144


def lower_inverse(gram):
    row_of = lax.broadcasted_iota(jnp.int32, (8, 128), 0)
    lane_of = lax.broadcasted_iota(jnp.int32, (8, 128), 1)
    blocks = []
    for g in range(8):
        eye = jnp.where(lane_of == row_of + (64 + 8 * g), 1.0, 0.0).astype(F32)
        blocks.append(jnp.concatenate([gram[8 * g : 8 * g + 8], eye[:, 64:]], axis=1))
    for k in range(RANK - 1):
        own, at = divmod(k, 8)
        row = blocks[own][at : at + 1, :]
        scaled = row / row[:, k : k + 1]
        for g in range(own, 8):
            col = blocks[g][:, k : k + 1]
            if g == own:
                col = jnp.where(row_of[:, 0:1] > at, col, 0.0)
            blocks[g] = blocks[g] - col * scaled
    out = []
    for g in range(8):
        pivot = jnp.sum(jnp.where(lane_of == row_of + 8 * g, blocks[g], 0.0), axis=1, keepdims=True)
        out.append(blocks[g][:, 64:] * (1.0 / jnp.sqrt(pivot)))
    return jnp.concatenate(out, axis=0)


def folded(block):
    n = block.shape[0] // 2
    return jnp.concatenate([block[0:n], block[n:]], axis=1)


def unfolded(block):
    return jnp.concatenate([block[:, 0:64], block[:, 64:128]], axis=0)


class RingSum:
    def __init__(self, remote, blocks, part, place, right, left, passing, arrived):
        self.blocks, self.part, self.place, self.passing, self.arrived = blocks, part, place, passing, arrived
        forward, backward = (left, right) if part else (right, left)
        self.ahead, behind = (place + (3 if part else 1)) % 4, (place + (1 if part else 3)) % 4
        self.across = remote(blocks.at[(place + 2) % 4, part], passing.at[part], forward)
        self.back = remote(blocks.at[behind, part], arrived.at[1, part], backward)
        self.on = remote(blocks.at[self.ahead, part], arrived.at[0, part], forward)

    def start(self):
        self.across.start()
        self.back.start()

    def forward(self):
        self.across.wait_recv()
        self.blocks[self.ahead, self.part] += self.passing[self.part]
        self.on.start()

    def total(self):
        self.back.wait_recv()
        self.on.wait_recv()
        return self.blocks[self.place, self.part] + self.arrived[0, self.part] + self.arrived[1, self.part]


def kernel(
    signal,
    sketch,
    basis,
    proj,
    sk_v,
    xr,
    uu,
    vv,
    vw,
    skl,
    ss,
    gs,
    gx,
    gy,
    gz,
    ya,
    yb,
    fa,
    fb,
    ra,
    rb,
    sa,
    sb,
    ra2,
    rb2,
    zp,
    rz,
    local_sem,
    send_sem,
    recv_sem,
    last_send,
    last_recv,
):
    z = lax.axis_index("tx")
    ty = lax.axis_index("ty")
    y = ty // 8
    x = (ty // 2) % 4
    core = ty % 2
    me = z * 32 + ty

    def along(offset):
        index = (me + offset + 256) % 256
        return (index // 32, index % 32)

    def x_peer(k):
        return (z, y * 8 + ((x + k + 4) % 4) * 2 + core)

    def y_peer(k):
        return (z, ((y + k + 4) % 4) * 8 + x * 2 + core)

    def z_peer(k):
        return ((z + k + 8) % 8, ty)

    other = ty + 1 - 2 * core
    twin = (z, other)

    def z_other(k):
        return ((z + k + 8) % 8, other)

    copies = []

    def remote(src, dst, device):
        i = len(copies)
        copies.append(pltpu.make_async_remote_copy(
            src_ref=src,
            dst_ref=dst,
            send_sem=send_sem.at[i],
            recv_sem=recv_sem.at[i],
            device_id=device,
            device_id_type=MESH,
        ))
        return copies[i]

    own_rows = pl.ds(pl.multiple_of(core * ROWS, ROWS), ROWS)
    own_ranks = pl.ds(pl.multiple_of(core * HALF, HALF), HALF)
    get_signal = pltpu.make_async_copy(signal, xr.at[0, own_rows], local_sem.at[0])
    get_sketch = pltpu.make_async_copy(sketch.at[own_ranks], sk_v, local_sem.at[1])
    get_signal.start()
    get_sketch.start()

    barrier = pltpu.get_barrier_semaphore()
    sources = [along(2 - core), twin]
    sources += [x_peer(-k) for k in range(1, 4)]
    sources += [y_peer(-k) for k in range(1, 4)]
    sources += [z_peer(-k) for k in range(1, 8)]
    sources += [z_other(-k) for k in range(1, 8)]
    for source in sources:
        pl.semaphore_signal(barrier, inc=1, device_id=source, device_id_type=MESH)
    pl.semaphore_wait(barrier, len(sources) - 1 + 2 * (1 - core))

    halo_rows = pl.ds(TIMES, 64)
    halo_near = remote(signal.at[pl.ds(0, 64)], xr.at[0, halo_rows], along(-1))
    halo_far = pltpu.make_async_remote_copy(
        src_ref=signal.at[pl.ds(0, 64)],
        dst_ref=xr.at[0, halo_rows],
        send_sem=local_sem.at[2],
        recv_sem=recv_sem.at[0],
        device_id=along(-2),
        device_id_type=MESH,
    )

    @pl.when(core == 0)
    def _():
        halo_near.start()
        halo_far.start()

    pair_copy = remote(signal, xr.at[0, own_rows], twin)
    pair_copy.start()

    for m in range(2):
        xr[m, 2112:2240] = jnp.zeros((128, CH), BF16)
    def shifted(start, blocks, rest):
        for i in range(blocks):
            at = pl.multiple_of(start + i * 128, 16)
            near = xr[0, pl.ds(at, 144)]
            xr[1, pl.ds(at, 128)] = near[8:136]

        at = pl.multiple_of(start + blocks * 128, 16)
        near = xr[0, pl.ds(at, rest + 16)]
        xr[1, pl.ds(at, rest)] = near[8 : 8 + rest]

    get_signal.wait()
    shifted(core * ROWS, 7, 112)

    get_sketch.wait()
    columns = jnp.concatenate(
        [
            jnp.concatenate([sk_v[:, (8 * q + j) * CH : (8 * q + j + 1) * CH] for q in range(8)], axis=1)
            for j in range(8)
        ],
        axis=0,
    )

    def sub_shifted(start, rows):
        moved = [xr[q % 2, pl.ds(pl.multiple_of(16 * (q // 2) + start, 16), rows)] for q in range(8)]
        uu[pl.ds(pl.multiple_of(start, 16), rows)] = lax.dot_general(
            jnp.concatenate(moved, axis=1), columns, NT, preferred_element_type=F32
        )

    sub_shifted(core * ROWS, 960)
    pair_copy.wait_recv()
    shifted(ROWS - ROWS * core - 16 * (1 - core), 7, 128)
    sub_shifted(960 - 960 * core, 1024)
    halo_near.wait_recv()

    @pl.when(me >= 254)
    def _():
        xr[0, halo_rows] = jnp.zeros((64, CH), BF16)

    near = xr[0, 2032:2128]
    xr[1, 2032:2112] = near[8:88]
    sub_shifted(1984, 80)

    vv[...] = uu[0:2056, 0:128] + uu[4:2060, 128:256]
    vw[...] = vv[0:2052] + pltpu.roll(vv[2:2054], 64, axis=1)
    group = lax.broadcasted_iota(jnp.int32, (512, 128), 1) // HALF
    merged = None
    for g in range(4):
        at = g * 512
        part = vw[at : at + 512] + pltpu.roll(vw[at + 1 : at + 513], 96, axis=1)
        merged = part if g == 0 else jnp.where(group == g, pltpu.roll(part, 32 * g, axis=1), merged)
    turned = merged.T
    for g in range(4):
        skl[core, :, g * 512 : g * 512 + 512] = turned[g * HALF : g * HALF + HALF]
    sketched_copy = remote(skl.at[core], skl.at[core], twin)
    sketched_copy.start()

    padded = jnp.concatenate([skl[core], jnp.zeros((HALF, DEPTH - TIMES), F32)], axis=1)
    for j in range(8):
        moved = padded if j == 0 else pltpu.roll(padded, j, axis=1)
        high = moved.astype(BF16)
        ss[j * HALF : j * HALF + HALF] = high
        ss[256 + j * HALF : 256 + j * HALF + HALF] = (moved - high.astype(F32)).astype(BF16)

    def products(z_to, into, x_first):
        for i in range(2):
            right = xr[i, 8 * z_to : 8 * z_to + DEPTH]
            both = jnp.dot(ss[...], right, preferred_element_type=F32)
            block = both[0:256] + both[256:512]
            at = slice(i * HALF, i * HALF + HALF)
            half = (z_to % 4) // 2
            for j in range(8):
                y_to = j // 2
                for x0 in range(2):
                    x_to = (j % 2) * 2 + x0
                    piece = block[j * HALF : j * HALF + HALF, x0 * 128 : x0 * 128 + 128]
                    if x_first:
                        into[x_to, half, y_to, at] = piece
                    else:
                        into[y_to, half, x_to, at] = piece

    a_one = [RingSum(remote, ya, part, x, x_peer(1), x_peer(-1), fa, ra) for part in range(2)]
    b_one = [RingSum(remote, yb, part, y, y_peer(1), y_peer(-1), fb, rb) for part in range(2)]
    products(0, ya, True)
    a_one[0].start()
    products(4, yb, False)
    b_one[0].start()

    products(2, ya, True)
    a_one[1].start()
    products(6, yb, False)
    b_one[1].start()

    sketched_copy.wait_recv()
    full = jnp.concatenate([skl[0], skl[1]], axis=0)
    high = full.astype(BF16)
    rest = full - high.astype(F32)
    middle = rest.astype(BF16)
    low = (rest - middle.astype(F32)).astype(BF16)
    terms = jnp.concatenate([high, middle, low], axis=0)
    both = lax.dot_general(terms, terms, NT, preferred_element_type=F32)
    rows = both[0:64] + (both[64:128] + both[128:192])
    gs[0] = folded(rows[:, 0:64] + (rows[:, 64:128] + rows[:, 128:192]))
    gram_x = [remote(gs.at[0], gx.at[k - 1], x_peer(k)) for k in range(1, 4)]
    for copy in gram_x:
        copy.start()

    a_one[0].forward()
    b_one[0].forward()
    for copy in gram_x:
        copy.wait_recv()
    gs[1] = gs[0] + gx[0] + gx[1] + gx[2]
    gram_y = [remote(gs.at[1], gy.at[k - 1], y_peer(k)) for k in range(1, 4)]
    for copy in gram_y:
        copy.start()
    a_one[1].forward()
    b_one[1].forward()

    def second(rings, sums, place, peer, landing):
        for ring in rings:
            sums[:, ring.part] = ring.total()
        sends = [remote(sums.at[(place + k) % 4], landing.at[k - 1], peer(k)) for k in (2, 1, 3)]
        for copy in sends:
            copy.start()
        return sends

    for copy in gram_y:
        copy.wait_recv()
    gs[2] = gs[1] + gy[0] + gy[1] + gy[2]
    gram_z = [remote(gs.at[2], gz.at[k - 1], z_peer(k)) for k in range(1, 8)]
    for copy in gram_z:
        copy.start()
    a_two = second(a_one, sa, y, y_peer, ra2)
    b_two = second(b_one, sb, x, x_peer, rb2)

    def pack(z_to, halves):
        for h in range(2):
            for i in range(2):
                piece = halves[h][i * HALF : i * HALF + HALF]
                for c in range(2):
                    zp[z_to + 2 * h + i, c] = folded(piece[:, c * 64 : c * 64 + 64])

    def along_z(z_to):
        k = (z_to - z + 8) % 8
        pair = []
        for which, device in ((0, (z_to, ty)), (1, (z_to, other))):
            pair.append(pltpu.make_async_remote_copy(
                src_ref=zp.at[z_to, (core + which) % 2],
                dst_ref=rz.at[which, k],
                send_sem=last_send.at[which, k],
                recv_sem=last_recv.at[which, k],
                device_id=device,
                device_id_type=MESH,
            ))
        return pair

    def send_along_z(first):
        for z_to in range(first, first + 4):
            same_core, other_core = along_z(z_to)

            @pl.when(z != z_to)
            def _():
                same_core.start()

            other_core.start()

    for copy in a_two:
        copy.wait_recv()
    pack(0, [sa[y, h] + ra2[0, h] + ra2[1, h] + ra2[2, h] for h in range(2)])
    send_along_z(0)
    for copy in b_two:
        copy.wait_recv()
    pack(4, [sb[x, h] + rb2[0, h] + rb2[1, h] + rb2[2, h] for h in range(2)])
    send_along_z(4)

    for copy in gram_z:
        copy.wait_recv()
    gram_sum = gs[2]
    for k in range(7):
        gram_sum = gram_sum + gz[k]
    inverse = lower_inverse(unfolded(gram_sum) * (1.0 / SAMPLES))
    ours = pl.ds(pl.multiple_of(core * ROWS, ROWS), ROWS)
    basis[...] = jnp.dot(
        inverse,
        jnp.concatenate([skl[0, :, ours], skl[1, :, ours]], axis=0),
        precision=HIGH,
        preferred_element_type=F32,
    )
    landed = [along_z((z + k) % 8) for k in range(8)]
    for k in range(8):
        if k > 0:
            landed[k][0].wait_recv()
        landed[k][1].wait_recv()
    own = zp[z, core]
    others = rz[1, 0]
    for k in range(1, 8):
        own = own + rz[0, k]
        others = others + rz[1, k]
    top = jnp.where(core == 0, own, others)
    bottom = jnp.where(core == 0, others, own)
    owned = jnp.concatenate([unfolded(top), unfolded(bottom)], axis=0)
    proj[...] = jnp.dot(inverse, owned, precision=HIGH, preferred_element_type=F32) * (1.0 / math.sqrt(SAMPLES))

    @pl.when(core == 0)
    def _():
        halo_near.wait_send()
        halo_far.wait_send()

    for copy in copies[1:]:
        copy.wait_send()
    for k in range(8):
        if k > 0:
            landed[k][0].wait_send()
        landed[k][1].wait_send()


COPIES = 3 + 3 + 3 + 7 + 4 * 3 + 2 * 3


def finish(basis, proj, basis_out, proj_out, sem):
    first = pltpu.make_async_copy(basis, basis_out, sem.at[0])
    second = pltpu.make_async_copy(proj, proj_out, sem.at[1])
    first.start()
    second.start()
    first.wait()
    second.wait()


def shards(signal, sketch):
    shapes = (
        jax.ShapeDtypeStruct((RANK, ROWS), F32),
        jax.ShapeDtypeStruct((RANK, 64), F32),
    )
    results = pl.pallas_call(
        kernel,
        out_shape=shapes,
        in_specs=[pl.BlockSpec(memory_space=pl.ANY)] * 2,
        out_specs=[pl.BlockSpec(memory_space=pltpu.VMEM)] * 2,
        scratch_shapes=[
            pltpu.VMEM((HALF, LAGS * CH), BF16),
            pltpu.VMEM((2, 2240, CH), BF16),
            pltpu.VMEM((2064, CH), F32),
            pltpu.VMEM((2056, 128), F32),
            pltpu.VMEM((2052, 128), F32),
            pltpu.VMEM((2, HALF, TIMES), F32),
            pltpu.VMEM((512, DEPTH), BF16),
            pltpu.VMEM((3, 32, 128), F32),
            pltpu.VMEM((3, 32, 128), F32),
            pltpu.VMEM((3, 32, 128), F32),
            pltpu.VMEM((7, 32, 128), F32),
            pltpu.VMEM((4, 2, 4, 64, 128), F32),
            pltpu.VMEM((4, 2, 4, 64, 128), F32),
            pltpu.VMEM((2, 4, 64, 128), F32),
            pltpu.VMEM((2, 4, 64, 128), F32),
            pltpu.VMEM((2, 2, 4, 64, 128), F32),
            pltpu.VMEM((2, 2, 4, 64, 128), F32),
            pltpu.VMEM((4, 2, 64, 128), F32),
            pltpu.VMEM((4, 2, 64, 128), F32),
            pltpu.VMEM((3, 2, 64, 128), F32),
            pltpu.VMEM((3, 2, 64, 128), F32),
            pltpu.VMEM((8, 2, 16, 128), F32),
            pltpu.VMEM((2, 8, 16, 128), F32),
            pltpu.SemaphoreType.DMA((3,)),
            pltpu.SemaphoreType.DMA((COPIES,)),
            pltpu.SemaphoreType.DMA((COPIES,)),
            pltpu.SemaphoreType.DMA((2, 8)),
            pltpu.SemaphoreType.DMA((2, 8)),
        ],
        compiler_params=pltpu.CompilerParams(
            collective_id=0, has_side_effects=True, vmem_limit_bytes=54784 * 1024
        ),
        name="range_finder",
    )(signal, sketch)
    return pl.pallas_call(
        finish,
        out_shape=shapes,
        in_specs=[pl.BlockSpec(memory_space=pltpu.VMEM)] * 2,
        out_specs=[pl.BlockSpec(memory_space=pltpu.HBM)] * 2,
        scratch_shapes=[pltpu.SemaphoreType.DMA((2,))],
        compiler_params=pltpu.CompilerParams(vmem_limit_bytes=2**20),
        name="write_results",
    )(*results)


def solution(mesh):
    in_specs = (P(("tx", "ty"), None), P())
    out_specs = (P(None, ("tx", "ty")), P(None, ("tx", "ty")))
    return jax.shard_map(shards, mesh=mesh, in_specs=in_specs, out_specs=out_specs, check_vma=False)
```

```python
import math

import jax
import jax.numpy as jnp
from jax import lax
from jax.experimental import pallas as pl
from jax.experimental.pallas import tpu as pltpu
from jax.sharding import PartitionSpec as P

MESH = pl.DeviceIdType.MESH
F32 = jnp.float32
BF16 = jnp.bfloat16
HIGH = lax.Precision.HIGHEST
NT = (((1,), (1,)), ((), ()))

ROWS = 1024
CH = 256
RANK = 64
LAGS = 64
HALF = 32
TIMES = 2048
DEPTH = 2304
SAMPLES = 262144


def lower_inverse(gram):
    row_of = lax.broadcasted_iota(jnp.int32, (8, 128), 0)
    lane_of = lax.broadcasted_iota(jnp.int32, (8, 128), 1)
    blocks = []
    for g in range(8):
        eye = jnp.where(lane_of == row_of + (64 + 8 * g), 1.0, 0.0).astype(F32)
        blocks.append(jnp.concatenate([gram[8 * g : 8 * g + 8], eye[:, 64:]], axis=1))
    for k in range(RANK - 1):
        own, at = divmod(k, 8)
        row = blocks[own][at : at + 1, :]
        scaled = row / row[:, k : k + 1]
        for g in range(own, 8):
            col = blocks[g][:, k : k + 1]
            if g == own:
                col = jnp.where(row_of[:, 0:1] > at, col, 0.0)
            blocks[g] = blocks[g] - col * scaled
    out = []
    for g in range(8):
        pivot = jnp.sum(jnp.where(lane_of == row_of + 8 * g, blocks[g], 0.0), axis=1, keepdims=True)
        out.append(blocks[g][:, 64:] * (1.0 / jnp.sqrt(pivot)))
    return jnp.concatenate(out, axis=0)


def folded(block):
    n = block.shape[0] // 2
    return jnp.concatenate([block[0:n], block[n:]], axis=1)


def unfolded(block):
    return jnp.concatenate([block[:, 0:64], block[:, 64:128]], axis=0)


class RingSum:
    def __init__(self, remote, blocks, part, place, right, left, passing, arrived):
        self.blocks, self.part, self.place, self.passing, self.arrived = blocks, part, place, passing, arrived
        forward, backward = (left, right) if part else (right, left)
        self.ahead, behind = (place + (3 if part else 1)) % 4, (place + (1 if part else 3)) % 4
        self.across = remote(blocks.at[(place + 2) % 4, part], passing.at[part], forward)
        self.back = remote(blocks.at[behind, part], arrived.at[1, part], backward)
        self.on = remote(blocks.at[self.ahead, part], arrived.at[0, part], forward)

    def start(self):
        self.across.start()
        self.back.start()

    def forward(self):
        self.across.wait_recv()
        self.blocks[self.ahead, self.part] += self.passing[self.part]
        self.on.start()

    def total(self):
        self.back.wait_recv()
        self.on.wait_recv()
        return self.blocks[self.place, self.part] + self.arrived[0, self.part] + self.arrived[1, self.part]


def kernel(
    signal,
    sketch,
    basis,
    proj,
    sk_v,
    xr,
    uu,
    vv,
    vw,
    skl,
    ss,
    gs,
    gx,
    gy,
    gz,
    ya,
    yb,
    fa,
    fb,
    ra,
    rb,
    sa,
    sb,
    ra2,
    rb2,
    zp,
    rz,
    local_sem,
    send_sem,
    recv_sem,
    last_send,
    last_recv,
):
    z = lax.axis_index("tx")
    ty = lax.axis_index("ty")
    y = ty // 8
    x = (ty // 2) % 4
    core = ty % 2
    me = z * 32 + ty

    def along(offset):
        index = (me + offset + 256) % 256
        return (index // 32, index % 32)

    def x_peer(k):
        return (z, y * 8 + ((x + k + 4) % 4) * 2 + core)

    def y_peer(k):
        return (z, ((y + k + 4) % 4) * 8 + x * 2 + core)

    def z_peer(k):
        return ((z + k + 8) % 8, ty)

    other = ty + 1 - 2 * core
    twin = (z, other)

    def z_other(k):
        return ((z + k + 8) % 8, other)

    copies = []

    def remote(src, dst, device):
        i = len(copies)
        copies.append(pltpu.make_async_remote_copy(
            src_ref=src,
            dst_ref=dst,
            send_sem=send_sem.at[i],
            recv_sem=recv_sem.at[i],
            device_id=device,
            device_id_type=MESH,
        ))
        return copies[i]

    own_rows = pl.ds(pl.multiple_of(core * ROWS, ROWS), ROWS)
    own_ranks = pl.ds(pl.multiple_of(core * HALF, HALF), HALF)
    get_signal = pltpu.make_async_copy(signal, xr.at[0, own_rows], local_sem.at[0])
    get_sketch = pltpu.make_async_copy(sketch.at[own_ranks], sk_v, local_sem.at[1])
    get_signal.start()
    get_sketch.start()

    barrier = pltpu.get_barrier_semaphore()
    sources = [along(2 - core), twin]
    sources += [x_peer(-k) for k in range(1, 4)]
    sources += [y_peer(-k) for k in range(1, 4)]
    sources += [z_peer(-k) for k in range(1, 8)]
    sources += [z_other(-k) for k in range(1, 8)]
    for source in sources:
        pl.semaphore_signal(barrier, inc=1, device_id=source, device_id_type=MESH)
    pl.semaphore_wait(barrier, len(sources) - 1 + 2 * (1 - core))

    halo_rows = pl.ds(TIMES, 64)
    halo_near = remote(signal.at[pl.ds(0, 64)], xr.at[0, halo_rows], along(-1))
    halo_far = pltpu.make_async_remote_copy(
        src_ref=signal.at[pl.ds(0, 64)],
        dst_ref=xr.at[0, halo_rows],
        send_sem=local_sem.at[2],
        recv_sem=recv_sem.at[0],
        device_id=along(-2),
        device_id_type=MESH,
    )

    @pl.when(core == 0)
    def _():
        halo_near.start()
        halo_far.start()

    pair_copy = remote(signal, xr.at[0, own_rows], twin)
    pair_copy.start()

    for m in range(2):
        xr[m, 2112:2368] = jnp.zeros((256, CH), BF16)
    def shifted(start, blocks, rest):
        for i in range(blocks):
            at = pl.multiple_of(start + i * 128, 16)
            near = xr[0, pl.ds(at, 144)]
            xr[1, pl.ds(at, 128)] = near[8:136]

        at = pl.multiple_of(start + blocks * 128, 16)
        near = xr[0, pl.ds(at, rest + 16)]
        xr[1, pl.ds(at, rest)] = near[8 : 8 + rest]

    get_signal.wait()
    shifted(core * ROWS, 7, 112)

    get_sketch.wait()
    columns = jnp.concatenate(
        [
            jnp.concatenate([sk_v[:, (8 * q + j) * CH : (8 * q + j + 1) * CH] for q in range(8)], axis=1)
            for j in range(8)
        ],
        axis=0,
    )

    def sub_shifted(start, rows):
        moved = [xr[q % 2, pl.ds(pl.multiple_of(16 * (q // 2) + start, 16), rows)] for q in range(8)]
        uu[pl.ds(pl.multiple_of(start, 16), rows)] = lax.dot_general(
            jnp.concatenate(moved, axis=1), columns, NT, preferred_element_type=F32
        )

    sub_shifted(core * ROWS, 960)
    pair_copy.wait_recv()
    shifted(ROWS - ROWS * core - 16 * (1 - core), 7, 128)
    sub_shifted(960 - 960 * core, 1024)
    halo_near.wait_recv()

    @pl.when(me >= 254)
    def _():
        xr[0, halo_rows] = jnp.zeros((64, CH), BF16)

    near = xr[0, 2032:2128]
    xr[1, 2032:2112] = near[8:88]
    sub_shifted(1984, 80)

    vv[...] = uu[0:2056, 0:128] + uu[4:2060, 128:256]
    vw[...] = vv[0:2052] + pltpu.roll(vv[2:2054], 64, axis=1)
    group = lax.broadcasted_iota(jnp.int32, (512, 128), 1) // HALF
    merged = None
    for g in range(4):
        at = g * 512
        part = vw[at : at + 512] + pltpu.roll(vw[at + 1 : at + 513], 96, axis=1)
        merged = part if g == 0 else jnp.where(group == g, pltpu.roll(part, 32 * g, axis=1), merged)
    turned = merged.T
    for g in range(4):
        skl[core, :, g * 512 : g * 512 + 512] = turned[g * HALF : g * HALF + HALF]
    sketched_copy = remote(skl.at[core], skl.at[core], twin)
    sketched_copy.start()

    padded = jnp.concatenate([skl[core], jnp.zeros((HALF, DEPTH - TIMES), F32)], axis=1)
    for j in range(8):
        moved = padded if j == 0 else pltpu.roll(padded, j, axis=1)
        high = moved.astype(BF16)
        ss[j * HALF : j * HALF + HALF] = high
        ss[256 + j * HALF : 256 + j * HALF + HALF] = (moved - high.astype(F32)).astype(BF16)

    def products(z_to, into, x_first):
        for i in range(2):
            right = xr[i, 8 * z_to : 8 * z_to + DEPTH]
            both = jnp.dot(ss[...], right, preferred_element_type=F32)
            block = both[0:256] + both[256:512]
            at = slice(i * HALF, i * HALF + HALF)
            half = (z_to % 4) // 2
            for j in range(8):
                y_to = j // 2
                for x0 in range(2):
                    x_to = (j % 2) * 2 + x0
                    piece = block[j * HALF : j * HALF + HALF, x0 * 128 : x0 * 128 + 128]
                    if x_first:
                        into[x_to, half, y_to, at] = piece
                    else:
                        into[y_to, half, x_to, at] = piece

    a_one = [RingSum(remote, ya, part, x, x_peer(1), x_peer(-1), fa, ra) for part in range(2)]
    b_one = [RingSum(remote, yb, part, y, y_peer(1), y_peer(-1), fb, rb) for part in range(2)]
    products(0, ya, True)
    a_one[0].start()
    products(4, yb, False)
    b_one[0].start()

    products(2, ya, True)
    a_one[1].start()
    products(6, yb, False)
    b_one[1].start()

    sketched_copy.wait_recv()
    full = jnp.concatenate([skl[0], skl[1]], axis=0)
    high = full.astype(BF16)
    rest = full - high.astype(F32)
    middle = rest.astype(BF16)
    low = (rest - middle.astype(F32)).astype(BF16)
    terms = jnp.concatenate([high, middle, low], axis=0)
    both = lax.dot_general(terms, terms, NT, preferred_element_type=F32)
    rows = both[0:64] + (both[64:128] + both[128:192])
    gs[0] = folded(rows[:, 0:64] + (rows[:, 64:128] + rows[:, 128:192]))
    gram_x = [remote(gs.at[0], gx.at[k - 1], x_peer(k)) for k in range(1, 4)]
    for copy in gram_x:
        copy.start()

    a_one[0].forward()
    b_one[0].forward()
    for copy in gram_x:
        copy.wait_recv()
    gs[1] = gs[0] + gx[0] + gx[1] + gx[2]
    gram_y = [remote(gs.at[1], gy.at[k - 1], y_peer(k)) for k in range(1, 4)]
    for copy in gram_y:
        copy.start()
    a_one[1].forward()
    b_one[1].forward()

    def second(rings, sums, place, peer, landing):
        for ring in rings:
            sums[:, ring.part] = ring.total()
        sends = [remote(sums.at[(place + k) % 4], landing.at[k - 1], peer(k)) for k in (2, 1, 3)]
        for copy in sends:
            copy.start()
        return sends

    for copy in gram_y:
        copy.wait_recv()
    gs[2] = gs[1] + gy[0] + gy[1] + gy[2]
    gram_z = [remote(gs.at[2], gz.at[k - 1], z_peer(k)) for k in range(1, 8)]
    for copy in gram_z:
        copy.start()
    a_two = second(a_one, sa, y, y_peer, ra2)
    b_two = second(b_one, sb, x, x_peer, rb2)

    def pack(z_to, halves):
        for h in range(2):
            for i in range(2):
                piece = halves[h][i * HALF : i * HALF + HALF]
                for c in range(2):
                    zp[z_to + 2 * h + i, c] = folded(piece[:, c * 64 : c * 64 + 64])

    def along_z(z_to):
        k = (z_to - z + 8) % 8
        pair = []
        for which, device in ((0, (z_to, ty)), (1, (z_to, other))):
            pair.append(pltpu.make_async_remote_copy(
                src_ref=zp.at[z_to, (core + which) % 2],
                dst_ref=rz.at[which, k],
                send_sem=last_send.at[which, k],
                recv_sem=last_recv.at[which, k],
                device_id=device,
                device_id_type=MESH,
            ))
        return pair

    def send_along_z(first):
        for z_to in range(first, first + 4):
            same_core, other_core = along_z(z_to)

            @pl.when(z != z_to)
            def _():
                same_core.start()

            other_core.start()

    for copy in a_two:
        copy.wait_recv()
    pack(0, [sa[y, h] + ra2[0, h] + ra2[1, h] + ra2[2, h] for h in range(2)])
    send_along_z(0)
    for copy in b_two:
        copy.wait_recv()
    pack(4, [sb[x, h] + rb2[0, h] + rb2[1, h] + rb2[2, h] for h in range(2)])
    send_along_z(4)

    for copy in gram_z:
        copy.wait_recv()
    gram_sum = gs[2]
    for k in range(7):
        gram_sum = gram_sum + gz[k]
    inverse = lower_inverse(unfolded(gram_sum) * (1.0 / SAMPLES))
    ours = pl.ds(pl.multiple_of(core * ROWS, ROWS), ROWS)
    basis[...] = jnp.dot(
        inverse,
        jnp.concatenate([skl[0, :, ours], skl[1, :, ours]], axis=0),
        precision=HIGH,
        preferred_element_type=F32,
    )
    landed = [along_z((z + k) % 8) for k in range(8)]
    for k in range(8):
        if k > 0:
            landed[k][0].wait_recv()
        landed[k][1].wait_recv()
    own = zp[z, core]
    others = rz[1, 0]
    for k in range(1, 8):
        own = own + rz[0, k]
        others = others + rz[1, k]
    top = jnp.where(core == 0, own, others)
    bottom = jnp.where(core == 0, others, own)
    owned = jnp.concatenate([unfolded(top), unfolded(bottom)], axis=0)
    proj[...] = jnp.dot(inverse, owned, precision=HIGH, preferred_element_type=F32) * (1.0 / math.sqrt(SAMPLES))

    @pl.when(core == 0)
    def _():
        halo_near.wait_send()
        halo_far.wait_send()

    for copy in copies[1:]:
        copy.wait_send()
    for k in range(8):
        if k > 0:
            landed[k][0].wait_send()
        landed[k][1].wait_send()


COPIES = 3 + 3 + 3 + 7 + 4 * 3 + 2 * 3


def finish(basis, proj, basis_out, proj_out, sem):
    first = pltpu.make_async_copy(basis, basis_out, sem.at[0])
    second = pltpu.make_async_copy(proj, proj_out, sem.at[1])
    first.start()
    second.start()
    first.wait()
    second.wait()


def shards(signal, sketch):
    shapes = (
        jax.ShapeDtypeStruct((RANK, ROWS), F32),
        jax.ShapeDtypeStruct((RANK, 64), F32),
    )
    results = pl.pallas_call(
        kernel,
        out_shape=shapes,
        in_specs=[pl.BlockSpec(memory_space=pl.ANY)] * 2,
        out_specs=[pl.BlockSpec(memory_space=pltpu.VMEM)] * 2,
        scratch_shapes=[
            pltpu.VMEM((HALF, LAGS * CH), BF16),
            pltpu.VMEM((2, 2368, CH), BF16),
            pltpu.VMEM((2064, CH), F32),
            pltpu.VMEM((2056, 128), F32),
            pltpu.VMEM((2052, 128), F32),
            pltpu.VMEM((2, HALF, TIMES), F32),
            pltpu.VMEM((512, DEPTH), BF16),
            pltpu.VMEM((3, 32, 128), F32),
            pltpu.VMEM((3, 32, 128), F32),
            pltpu.VMEM((3, 32, 128), F32),
            pltpu.VMEM((7, 32, 128), F32),
            pltpu.VMEM((4, 2, 4, 64, 128), F32),
            pltpu.VMEM((4, 2, 4, 64, 128), F32),
            pltpu.VMEM((2, 4, 64, 128), F32),
            pltpu.VMEM((2, 4, 64, 128), F32),
            pltpu.VMEM((2, 2, 4, 64, 128), F32),
            pltpu.VMEM((2, 2, 4, 64, 128), F32),
            pltpu.VMEM((4, 2, 64, 128), F32),
            pltpu.VMEM((4, 2, 64, 128), F32),
            pltpu.VMEM((3, 2, 64, 128), F32),
            pltpu.VMEM((3, 2, 64, 128), F32),
            pltpu.VMEM((8, 2, 16, 128), F32),
            pltpu.VMEM((2, 8, 16, 128), F32),
            pltpu.SemaphoreType.DMA((3,)),
            pltpu.SemaphoreType.DMA((COPIES,)),
            pltpu.SemaphoreType.DMA((COPIES,)),
            pltpu.SemaphoreType.DMA((2, 8)),
            pltpu.SemaphoreType.DMA((2, 8)),
        ],
        compiler_params=pltpu.CompilerParams(
            collective_id=0, has_side_effects=True, vmem_limit_bytes=54784 * 1024
        ),
        name="range_finder",
    )(signal, sketch)
    return pl.pallas_call(
        finish,
        out_shape=shapes,
        in_specs=[pl.BlockSpec(memory_space=pltpu.VMEM)] * 2,
        out_specs=[pl.BlockSpec(memory_space=pltpu.HBM)] * 2,
        scratch_shapes=[pltpu.SemaphoreType.DMA((2,))],
        compiler_params=pltpu.CompilerParams(vmem_limit_bytes=2**20),
        name="write_results",
    )(*results)


def solution(mesh):
    in_specs = (P(("tx", "ty"), None), P())
    out_specs = (P(None, ("tx", "ty")), P(None, ("tx", "ty")))
    return jax.shard_map(shards, mesh=mesh, in_specs=in_specs, out_specs=out_specs, check_vma=False)
```
